256 devices in a mesh: batch: 4 (over y_lo, core), cand: 64 (over y_hi, x, z).
Axes of the slice: x: 4, y: 4 (y_hi: 2, y_lo: 2; y = y_hi * 2 + y_lo), z: 8, core: 2. Of those that a mesh axis runs over, the one named last changes fastest.
Arguments:
- queries: bfloat16 [16384, 128], P(('batch', 'cand')), may hold values from -8 to 8
- candidates: bfloat16 [131072, 128], P(('batch', 'cand')), may hold values from -2 to 2
- positive: int32 [16384], P(('batch', 'cand')), may hold values from 0 to 131071
- bucket: int32 [131072], P(('batch', 'cand')), may hold values from 0 to 1023
- query_weight: bfloat16 [16384], P(('batch', 'cand')), may hold values from 0.5 to 2
- log_freq: float32 [1024], replicated, may hold values from -1 to 0
Outputs:
- query_grad: float32 [16384, 128], P(('batch', 'cand'))
- cand_grad: float32 [131072, 128], P(('batch', 'cand'))
The draws below stay inside these ranges and needn't reach their ends.
All inputs are finite; a program needn't handle non-finite values.
Results may differ from the reference program's by a relative error of at most 0.0019.
Values may be sent and summed in bfloat16 or wider, within the bound.
No kernel may reach another device: no remote copies, remote signals or barrier semaphores. Data moves between devices by JAX's collectives and lax.ppermute only.
A program may use at most 192 MiB of HBM per device.

```python
import math
import jax
import jax.numpy as jnp
from jax import lax

E = 128
NBUCKET = 1024
QUERIES = 16384
CANDS = 131072


def draw_queries(key, part):
    key = jax.random.fold_in(key, 1)
    values = jax.random.truncated_normal(key, -6.0, 6.0, (QUERIES, E), jnp.float32)
    return values.astype(jnp.bfloat16)


def draw_candidates(key, part):
    key = jax.random.fold_in(key, 3)
    values = 0.3 * jax.random.truncated_normal(key, -6.0, 6.0, (CANDS, E), jnp.float32)
    return values.astype(jnp.bfloat16)


def touch_ends(drawn, stream_key, smallest, largest):
    index_at = [jax.random.randint(jax.random.fold_in(stream_key, axis), (), 0, length) for axis, length in enumerate(drawn.shape)]
    widest = drawn.shape.index(max(drawn.shape))
    beside = index_at[:widest] + [(index_at[widest] + 1) % drawn.shape[widest]] + index_at[widest + 1:]
    return drawn.at[tuple(index_at)].set(smallest).at[tuple(beside)].set(largest)


def shard_levels(stream_key, extent, shards, least, top_value):
    def one(position, blocks):
        steps = jax.random.uniform(jax.random.fold_in(jax.random.fold_in(stream_key, 6), position), (blocks,), jnp.float32, least / len(shards), top_value / len(shards))
        return jnp.repeat(jnp.exp(steps), extent[position] // blocks).reshape((-1,) + (1,) * (len(extent) - position - 1))

    loudness = one(*shards[0])
    for cut in shards[1:]:
        loudness = loudness * one(*cut)
    return loudness


def setup_inputs(seed: int = 0) -> dict:
    splits = jax.random.split(jax.random.key(seed), 7)
    return {
        "queries": draw_queries(jax.random.fold_in(splits[6], 71), 0),
        "candidates": draw_candidates(jax.random.fold_in(splits[6], 71), 0),
        "positive": touch_ends(jax.random.randint(splits[2], (QUERIES,), 0, CANDS), jax.random.fold_in(splits[2], 1), 0, CANDS - 1).astype(jnp.int32),
        "bucket": touch_ends(jax.random.randint(splits[3], (CANDS,), 0, NBUCKET), jax.random.fold_in(splits[3], 1), 0, NBUCKET - 1).astype(jnp.int32),
        "query_weight": jnp.clip(jnp.exp(math.log(2.0) - 1.3862944 * jax.random.uniform(splits[4], (QUERIES,), jnp.float32) ** shard_levels(splits[4], (QUERIES,), ((0, 256),), -0.2, 0.2)), 0.5, 2.0).astype(jnp.bfloat16),
        "log_freq": jnp.clip(jax.random.uniform(splits[5], (NBUCKET,), jnp.float32, -1.0, 0.0), -1.0, 0.0),
    }


def reference(queries, candidates, positive, bucket, query_weight, log_freq):
    shift = log_freq[bucket]
    count_cands = candidates.shape[0]
    feature_dim = candidates.shape[1]
    column_index = jnp.arange(count_cands, dtype=jnp.int32)
    block_size = min(256, queries.shape[0])
    block_count = queries.shape[0] // block_size

    def one_block(carry_grad, pieces):
        query_block, index_block, weight_block = pieces
        logits = jnp.dot(query_block, candidates.T, preferred_element_type=jnp.float32) - shift[None, :]
        row_max = jnp.max(logits, axis=1, keepdims=True)
        expo = jnp.exp(logits - row_max)
        row_total = jnp.sum(expo, axis=1, keepdims=True)
        matched = (column_index[None, :] == index_block[:, None]).astype(jnp.float32)
        grad = (weight_block.astype(jnp.float32)[:, None] * (expo / row_total - matched)).astype(jnp.bfloat16)
        query_part = jnp.dot(grad, candidates, preferred_element_type=jnp.float32)
        carry_grad = carry_grad + jnp.dot(grad.T, query_block, preferred_element_type=jnp.float32)
        return carry_grad, query_part

    start_grad = jnp.zeros((count_cands, feature_dim), jnp.float32)
    cand_grad, query_parts = lax.scan(
        one_block,
        start_grad,
        (queries.reshape(block_count, block_size, feature_dim),
         positive.reshape(block_count, block_size),
         query_weight.reshape(block_count, block_size)))
    return query_parts.reshape(-1, feature_dim), cand_grad
```

```python
import functools

import jax
import jax.numpy as jnp
from jax import lax
from jax.experimental import pallas as pl
from jax.experimental.pallas import tpu as pltpu
from jax.sharding import Mesh, PartitionSpec as P

bf16 = jnp.bfloat16
f32 = jnp.float32
i32 = jnp.int32
NT = (((1,), (1,)), ((), ()))
NN = (((1,), (0,)), ((), ()))
TN = (((0,), (0,)), ((), ()))
AXES = ("yl", "c", "yh", "x", "z")
GROUP = ("x", "z")
RING = ("yl", "yh")
NY, NCORE, NGROUP = 4, 2, 32
VMEM = pl.BlockSpec(memory_space=pltpu.VMEM)
SMEM = pl.BlockSpec(memory_space=pltpu.SMEM)
E = 128
QB = 64
CB = 512
QPAD = 16
CPAD = 16
SIDE = 32
NQ = NGROUP * QB
HALF = NY * CB
NC = NCORE * HALF


def stats_kernel(here, table, q_in, own, other, c_ext, q_ext, aux, lse_out, meta):
    lane = lax.broadcasted_iota(i32, (SIDE, E), 1)
    row = lax.broadcasted_iota(i32, (SIDE, E), 0)
    freq = table[...]
    high = freq.astype(bf16).astype(f32)
    rest = freq - high
    middle = rest.astype(bf16).astype(f32)
    low = rest - middle
    parts = jnp.where(
        lane < SIDE, high, jnp.where(lane < 2 * SIDE, middle, jnp.where(lane < 3 * SIDE, low, 0.0))
    ).astype(bf16)
    pick = ((lane & (SIDE - 1)) == row).astype(f32).astype(bf16)

    for core, block_ref in enumerate((own, other)):
        for s in range(NY):
            first = core * HALF + s * CB
            c_ext[first : first + CB, :E] = block_ref[s, :CB, :]
            codes = block_ref[s, CB : CB + CPAD, :].astype(f32)
            for r in range(CB // E):
                major = codes[r : r + 1, :].astype(i32)
                minor = codes[4 + r : 5 + r, :].astype(i32)
                hot_major = (row == major).astype(f32).astype(bf16)
                hot_minor = (row == minor).astype(f32).astype(bf16)
                values = lax.dot_general(hot_major, parts, TN, preferred_element_type=f32)
                mask = lax.dot_general(hot_minor, pick, TN, preferred_element_type=f32)
                c_ext[first + r * E : first + (r + 1) * E, E:] = (-(values * mask)).astype(bf16)

    wide = lax.broadcasted_iota(i32, (8, E), 1)
    for k in range(NGROUP):
        q_ext[k * QB : (k + 1) * QB, :E] = q_in[k, :QB, :]
    q_ext[:, E:] = jnp.ones((NQ, E), bf16)
    for t in range(NGROUP // 2):
        even = q_in[2 * t, QB : QB + QPAD, :].astype(f32)[:8]
        odd = q_in[2 * t + 1, QB : QB + QPAD, :].astype(f32)[:8]
        meta[:, t * E : (t + 1) * E] = jnp.where(wide < QB, even, odd)
    weight = meta[0:1, :]
    position = (meta[1:2, :] * 4096.0 + meta[2:3, :] * 64.0 + meta[3:4, :]).astype(i32)
    block = position >> 9
    y_there = ((block >> 5) & 1) * 2 + ((block >> 7) & 1)
    c_there = (block >> 6) & 1
    slot = (c_there ^ here[1]) * NY + ((here[0] - y_there) & 3)
    local = jnp.where((block & 31) == here[2], slot * CB + (position & (CB - 1)), -1)
    aux[2:3, :] = weight
    aux[3:4, :] = local.astype(f32)

    rows = 256
    queries = q_ext[...]

    def chunk(k, carry):
        top, total = carry
        start = pl.multiple_of(k * rows, rows)
        logits = lax.dot_general(c_ext[pl.ds(start, rows), :], queries, NT, preferred_element_type=f32)
        tall = logits.reshape(rows // 8, 8, NQ)
        new = jnp.maximum(top, jnp.max(tall, axis=0))
        total = total * jnp.exp(top - new) + jnp.sum(jnp.exp(tall - new[None]), axis=0)
        return new, total

    top, total = lax.fori_loop(
        0,
        NC // rows,
        chunk,
        (jnp.full((8, NQ), -jnp.inf, f32), jnp.zeros((8, NQ), f32)),
        unroll=4,
    )
    best = jnp.max(top, axis=0, keepdims=True)
    total = jnp.sum(total * jnp.exp(top - best), axis=0, keepdims=True)
    aux[0:1, :] = best
    aux[1:2, :] = total
    aux[4:8, :] = jnp.zeros((4, NQ), f32)
    lse = best + jnp.log(total)
    tile = jnp.concatenate([lse[:, t * E : (t + 1) * E] for t in range(NQ // E)], axis=0)
    for k in range(NGROUP):
        lse_out[k] = tile


def grad_kernel(base, last, here, c_ext, q_ext, aux, lse_all, *refs):
    if last:
        before, u_out, g_out, acc = refs
    else:
        u_out, g_out, acc = refs
    best = aux[0:1, :]
    weight = aux[2:3, :]
    local = aux[3:4, :].astype(i32)
    theirs = lse_all[...]
    mine = jnp.concatenate([best[:, t * E : (t + 1) * E] for t in range(NQ // E)], axis=0)
    member = lax.broadcasted_iota(i32, (NGROUP, NQ // E, E), 0)
    others = jnp.sum(jnp.where(member == here[2], 0.0, jnp.exp(theirs - mine[None])), axis=0)
    others = jnp.concatenate([others[t : t + 1, :] for t in range(NQ // E)], axis=1)
    scale = weight / (aux[1:2, :] + others)
    rows = 512
    queries = q_ext[...]
    narrow = q_ext[:, :E]
    if last:
        acc[...] = before[...]
    else:
        acc[...] = jnp.zeros_like(acc)

    def chunk(k, carry):
        start = pl.multiple_of(k * rows, rows)
        block = c_ext[pl.ds(base + start, rows), :]
        logits = lax.dot_general(block, queries, NT, preferred_element_type=f32)
        expo = jnp.exp(logits - best) * scale
        matched = lax.broadcasted_iota(i32, (rows, NQ), 0) == (local - (base + start))
        grad = (expo - jnp.where(matched, weight, 0.0)).astype(bf16)
        g_out[k] = lax.dot_general(grad, narrow, NN, preferred_element_type=f32)
        acc[...] += lax.dot_general(block[:, :E].T, grad, NN, preferred_element_type=f32)
        return carry

    lax.fori_loop(0, HALF // rows, chunk, 0)
    if last:
        u_out[...] = acc[...].T
    else:
        u_out[...] = acc[...]


def ring(step):
    place = [(y & 1) * 2 + (y >> 1) for y in range(NY)]
    return [(place[y], place[(y + step) % NY]) for y in range(NY)]


def shaped(shape, dtype):
    return jax.ShapeDtypeStruct(shape, dtype)


PARAMS = pltpu.CompilerParams(vmem_limit_bytes=48 * 2**20)


def per_device(queries, candidates, positive, bucket, query_weight, log_freq):
    y = lax.axis_index("yh") * 2 + lax.axis_index("yl")
    here = jnp.stack([y, lax.axis_index("c"), lax.axis_index(GROUP)]).astype(i32)

    codes = jnp.concatenate([bucket >> 5, bucket & 31]).astype(bf16).reshape(8, E)
    c_block = jnp.concatenate([candidates, codes, jnp.zeros((CPAD - 8, E), bf16)])
    spread = [c_block]
    for s in range(1, NY):
        spread.append(lax.ppermute(c_block, RING, ring(s)))
    own = jnp.stack(spread)
    swap = [(0, 1), (1, 0)]
    other = lax.ppermute(own, "c", swap)

    notes = jnp.stack(
        [
            query_weight,
            (positive >> 12).astype(bf16),
            ((positive >> 6) & 63).astype(bf16),
            (positive & 63).astype(bf16),
        ]
    )
    notes = jnp.concatenate([notes, notes], axis=1)
    q_block = jnp.concatenate([queries, notes, jnp.zeros((QPAD - 4, E), bf16)])
    q_in = lax.all_to_all(
        jnp.broadcast_to(q_block[None], (NGROUP, QB + QPAD, E)), GROUP, 0, 0, tiled=True
    )
    table = jnp.tile(log_freq.reshape(SIDE, SIDE), (1, 4))

    c_ext, q_ext, aux, lse = pl.pallas_call(
        stats_kernel,
        out_shape=[
            shaped((NC, 2 * E), bf16),
            shaped((NQ, 2 * E), bf16),
            shaped((8, NQ), f32),
            shaped((NGROUP, NQ // E, E), f32),
        ],
        in_specs=[SMEM] + [VMEM] * 4,
        out_specs=[VMEM] * 4,
        scratch_shapes=[pltpu.VMEM((8, NQ), f32)],
        compiler_params=PARAMS,
        name="stats",
    )(here, table, q_in, own, other)
    lse_all = lax.all_to_all(lse, GROUP, 0, 0, tiled=True)

    u_part, g_other = pl.pallas_call(
        functools.partial(grad_kernel, HALF, False),
        out_shape=[shaped((E, NQ), f32), shaped((NY, CB, E), f32)],
        in_specs=[SMEM] + [VMEM] * 4,
        out_specs=[VMEM] * 2,
        scratch_shapes=[pltpu.VMEM((E, NQ), f32)],
        compiler_params=PARAMS,
        name="grad_other",
    )(here, c_ext, q_ext, aux, lse_all)
    g_came = lax.ppermute(g_other, "c", swap)
    u_all, g_own = pl.pallas_call(
        functools.partial(grad_kernel, 0, True),
        out_shape=[shaped((NQ, E), f32), shaped((NY, CB, E), f32)],
        in_specs=[SMEM] + [VMEM] * 5,
        out_specs=[VMEM] * 2,
        scratch_shapes=[pltpu.VMEM((E, NQ), f32)],
        compiler_params=PARAMS,
        name="grad_own",
    )(here, c_ext, q_ext, aux, lse_all, u_part)

    g_sum = g_own + g_came
    pieces = [g_sum[0]]
    for s in range(1, NY):
        pieces.append(lax.ppermute(g_sum[s], RING, ring(-s)))
    u_in = lax.all_to_all(u_all.reshape(NGROUP, QB, E), GROUP, 0, 0, tiled=True)
    query_grad = jnp.sum(u_in, axis=0)
    cand_grad = (pieces[0] + pieces[1]) + (pieces[2] + pieces[3])
    return query_grad, cand_grad


def solution(mesh):
    fine = Mesh(mesh.devices.reshape(2, 2, 2, 4, 8), AXES)
    split = P(AXES)
    in_specs = (P(AXES, None), P(AXES, None), split, split, split, P())
    out_specs = (P(AXES, None), P(AXES, None))
    return jax.shard_map(
        per_device, mesh=fine, in_specs=in_specs, out_specs=out_specs, check_vma=False
    )
```

```python
import functools

import jax
import jax.numpy as jnp
from jax import lax
from jax.experimental import pallas as pl
from jax.experimental.pallas import tpu as pltpu
from jax.sharding import Mesh, PartitionSpec as P

bf16 = jnp.bfloat16
f32 = jnp.float32
i32 = jnp.int32
NT = (((1,), (1,)), ((), ()))
NN = (((1,), (0,)), ((), ()))
TN = (((0,), (0,)), ((), ()))
AXES = ("yl", "c", "yh", "x", "z")
GROUP = ("x", "z")
RING = ("yl", "yh")
NY, NX, NZ, NCORE = 4, 4, 8, 2
NGROUP = NX * NZ
VMEM = pl.BlockSpec(memory_space=pltpu.VMEM)
SMEM = pl.BlockSpec(memory_space=pltpu.SMEM)
E = 128
QB = 64
CB = 512
QPAD = 16
CPAD = 16
SIDE = 32
NQ = NGROUP * QB
HALF = NY * CB
QUART = NZ * QB
NC = NCORE * HALF


def stats_kernel(here, table, q0, q1, q2, q3, own, other, c_ext, q_ext, aux, lse_out, meta):
    lane = lax.broadcasted_iota(i32, (SIDE, E), 1)
    row = lax.broadcasted_iota(i32, (SIDE, E), 0)
    freq = table[...]
    high = freq.astype(bf16).astype(f32)
    rest = freq - high
    middle = rest.astype(bf16).astype(f32)
    low = rest - middle
    parts = jnp.where(
        lane < SIDE, high, jnp.where(lane < 2 * SIDE, middle, jnp.where(lane < 3 * SIDE, low, 0.0))
    ).astype(bf16)
    pick = ((lane & (SIDE - 1)) == row).astype(f32).astype(bf16)

    for core, block_ref in enumerate((own, other)):
        for s in range(NY):
            first = core * HALF + s * CB
            c_ext[first : first + CB, :E] = block_ref[s, :CB, :]
            codes = block_ref[s, CB : CB + CPAD, :].astype(f32)
            for r in range(CB // E):
                major = codes[r : r + 1, :].astype(i32)
                minor = codes[4 + r : 5 + r, :].astype(i32)
                hot_major = (row == major).astype(f32).astype(bf16)
                hot_minor = (row == minor).astype(f32).astype(bf16)
                values = lax.dot_general(hot_major, parts, TN, preferred_element_type=f32)
                mask = lax.dot_general(hot_minor, pick, TN, preferred_element_type=f32)
                c_ext[first + r * E : first + (r + 1) * E, E:] = (-(values * mask)).astype(bf16)

    wide = lax.broadcasted_iota(i32, (8, E), 1)
    q_ext[:, E:] = jnp.ones((NQ, E), bf16)
    for s, q_in in enumerate((q0, q1, q2, q3)):
        first = pl.multiple_of(((here[2] >> 3) - s & 3) * QUART, QUART)
        for k in range(NZ):
            q_ext[pl.ds(first + k * QB, QB), :E] = q_in[k, :QB, :]
        for t in range(NZ // 2):
            even = q_in[2 * t, QB : QB + QPAD, :].astype(f32)[:8]
            odd = q_in[2 * t + 1, QB : QB + QPAD, :].astype(f32)[:8]
            meta[:, pl.ds(first + t * E, E)] = jnp.where(wide < QB, even, odd)
    weight = meta[0:1, :]
    position = (meta[1:2, :] * 4096.0 + meta[2:3, :] * 64.0 + meta[3:4, :]).astype(i32)
    block = position >> 9
    y_there = ((block >> 5) & 1) * 2 + ((block >> 7) & 1)
    c_there = (block >> 6) & 1
    slot = (c_there ^ here[1]) * NY + ((here[0] - y_there) & 3)
    local = jnp.where((block & 31) == here[2], slot * CB + (position & (CB - 1)), -1)
    aux[2:3, :] = weight
    aux[3:4, :] = local.astype(f32)

    rows = 256
    queries = q_ext[...]

    def chunk(k, carry):
        top, total = carry
        start = pl.multiple_of(k * rows, rows)
        logits = lax.dot_general(c_ext[pl.ds(start, rows), :], queries, NT, preferred_element_type=f32)
        tall = logits.reshape(rows // 8, 8, NQ)
        new = jnp.maximum(top, jnp.max(tall, axis=0))
        total = total * jnp.exp(top - new) + jnp.sum(jnp.exp(tall - new[None]), axis=0)
        return new, total

    top, total = lax.fori_loop(
        0,
        NC // rows,
        chunk,
        (jnp.full((8, NQ), -jnp.inf, f32), jnp.zeros((8, NQ), f32)),
        unroll=4,
    )
    best = jnp.max(top, axis=0, keepdims=True)
    total = jnp.sum(total * jnp.exp(top - best), axis=0, keepdims=True)
    aux[0:1, :] = best
    aux[1:2, :] = total
    aux[4:8, :] = jnp.zeros((4, NQ), f32)
    lse = best + jnp.log(total)
    tile = jnp.concatenate([lse[:, t * E : (t + 1) * E] for t in range(NQ // E)], axis=0)
    for k in range(NGROUP):
        lse_out[k] = tile


def row_scale(here, aux, lse_all, first, count):
    best = aux[0:1, pl.ds(first, count)]
    tiles = count // E
    if count == NQ:
        theirs = lse_all[...]
    else:
        theirs = jnp.concatenate(
            [lse_all[k, pl.ds(first // E, tiles), :][None] for k in range(NGROUP)], axis=0
        )
    mine = jnp.concatenate([best[:, t * E : (t + 1) * E] for t in range(tiles)], axis=0)
    member = lax.broadcasted_iota(i32, (NGROUP, tiles, E), 0)
    others = jnp.sum(jnp.where(member == here[2], 0.0, jnp.exp(theirs - mine[None])), axis=0)
    others = jnp.concatenate([others[t : t + 1, :] for t in range(tiles)], axis=1)
    weight = aux[2:3, pl.ds(first, count)]
    return weight / (aux[1:2, pl.ds(first, count)] + others)


def grad_chunk(c_ext, row, rows, queries, narrow, best, scale, weight, local):
    block = c_ext[row : row + rows, :]
    logits = lax.dot_general(block, queries, NT, preferred_element_type=f32)
    expo = jnp.exp(logits - best) * scale
    matched = lax.broadcasted_iota(i32, logits.shape, 0) == (local - row)
    grad = (expo - jnp.where(matched, weight, 0.0)).astype(bf16)
    g_part = lax.dot_general(grad, narrow, NN, preferred_element_type=f32)
    u_part = lax.dot_general(block[:, :E].T, grad, NN, preferred_element_type=f32)
    return g_part, u_part


def other_kernel(here, c_ext, q_ext, aux, lse_all, u_out, g_out, aux_out):
    scale = row_scale(here, aux, lse_all, 0, NQ)
    aux_out[0:1, :] = aux[0:1, :]
    aux_out[1:2, :] = scale
    aux_out[2:8, :] = aux[2:8, :]
    queries = q_ext[...]
    total = None
    for k in range(HALF // CB):
        g_part, u_part = grad_chunk(
            c_ext, HALF + k * CB, CB, queries, queries[:, :E], aux[0:1, :], scale, aux[2:3, :],
            aux[3:4, :].astype(i32),
        )
        g_out[k] = g_part
        total = u_part if total is None else total + u_part
        u_out[...] = total


def own_kernel(shift, here, c_ext, q_ext, aux, before, *refs):
    g_in = refs[0] if len(refs) == 3 else None
    u_out, g_out = refs[-2:]
    first = pl.multiple_of(((here[2] >> 3) - shift & 3) * QUART, QUART)
    span = pl.ds(first, QUART)
    queries = q_ext[span, :]
    total = before[:, span]
    best, scale, weight = aux[0:1, span], aux[1:2, span], aux[2:3, span]
    local = aux[3:4, span].astype(i32)
    for k in range(HALF // CB):
        g_part, u_part = grad_chunk(
            c_ext, k * CB, CB, queries, queries[:, :E], best, scale, weight, local
        )
        g_out[k] = g_part if g_in is None else g_in[k] + g_part
        total = total + u_part
    u_out[...] = total.T


def ring(step):
    place = [(y & 1) * 2 + (y >> 1) for y in range(NY)]
    return [(place[y], place[(y + step) % NY]) for y in range(NY)]


def shaped(shape, dtype):
    return jax.ShapeDtypeStruct(shape, dtype)


def cost(pairs, products):
    return pl.CostEstimate(
        flops=2 * pairs * E * products * 2, bytes_accessed=8 * pairs, transcendentals=pairs
    )


PARAMS = pltpu.CompilerParams(vmem_limit_bytes=48 * 2**20)


def per_device(queries, candidates, positive, bucket, query_weight, log_freq):
    y = lax.axis_index("yh") * 2 + lax.axis_index("yl")
    here = jnp.stack([y, lax.axis_index("c"), lax.axis_index(GROUP)]).astype(i32)

    codes = jnp.concatenate([bucket >> 5, bucket & 31]).astype(bf16).reshape(8, E)
    c_block = jnp.concatenate([candidates, codes, jnp.zeros((CPAD - 8, E), bf16)])
    spread = [c_block]
    for s in range(1, NY):
        spread.append(lax.ppermute(c_block, RING, ring(s)))
    own = jnp.stack(spread)
    swap = [(0, 1), (1, 0)]
    other = lax.ppermute(own, "c", swap)

    notes = jnp.stack(
        [
            query_weight,
            (positive >> 12).astype(bf16),
            ((positive >> 6) & 63).astype(bf16),
            (positive & 63).astype(bf16),
        ]
    )
    notes = jnp.concatenate([notes, notes], axis=1)
    q_block = jnp.concatenate([queries, notes, jnp.zeros((QPAD - 4, E), bf16)])
    q_line = lax.all_to_all(
        jnp.broadcast_to(q_block[None], (NZ, QB + QPAD, E)), "z", 0, 0, tiled=True
    )
    q_in = [q_line]
    for s in range(1, NX):
        q_in.append(lax.ppermute(q_line, "x", [(i, (i + s) % NX) for i in range(NX)]))
    table = jnp.tile(log_freq.reshape(SIDE, SIDE), (1, 4))

    c_ext, q_ext, aux, lse = pl.pallas_call(
        stats_kernel,
        out_shape=[
            shaped((NC, 2 * E), bf16),
            shaped((NQ, 2 * E), bf16),
            shaped((8, NQ), f32),
            shaped((NGROUP, NQ // E, E), f32),
        ],
        in_specs=[SMEM] + [VMEM] * 7,
        out_specs=[VMEM] * 4,
        scratch_shapes=[pltpu.VMEM((8, NQ), f32)],
        compiler_params=PARAMS,
        cost_estimate=cost(NQ * NC, 1),
        name="stats",
    )(here, table, *q_in, own, other)
    lse_all = lax.all_to_all(lse, GROUP, 0, 0, tiled=True)

    u_part, g_other, aux = pl.pallas_call(
        other_kernel,
        out_shape=[shaped((E, NQ), f32), shaped((NY, CB, E), f32), shaped((8, NQ), f32)],
        in_specs=[SMEM] + [VMEM] * 4,
        out_specs=[VMEM] * 3,
        compiler_params=PARAMS,
        cost_estimate=cost(NQ * HALF, 3),
        name="grad_other",
    )(here, c_ext, q_ext, aux, lse_all)
    g_came = lax.ppermute(g_other, "c", swap)
    g_own = []
    u_sum = []
    for shift in (2, 1, 3, 0):
        u_piece, g_next = pl.pallas_call(
            functools.partial(own_kernel, shift),
            out_shape=[shaped((QUART, E), f32), shaped((NY, CB, E), f32)],
            in_specs=[SMEM] + [VMEM] * (4 + len(g_own)),
            out_specs=[VMEM] * 2,
            input_output_aliases={5: 1} if g_own else {},
            compiler_params=PARAMS,
            cost_estimate=cost(QUART * HALF, 3),
            name="grad_own",
        )(here, c_ext, q_ext, aux, u_part, *g_own)
        g_own = [g_next]
        if shift:
            u_piece = lax.ppermute(u_piece, "x", [(i, (i - shift) % NX) for i in range(NX)])
        u_sum.append(u_piece)

    g_sum = g_own[0] + g_came
    pieces = [g_sum[0]]
    for s in range(1, NY):
        pieces.append(lax.ppermute(g_sum[s], RING, ring(-s)))
    u_line = (u_sum[0] + u_sum[1]) + (u_sum[2] + u_sum[3])
    u_in = lax.all_to_all(u_line.reshape(NZ, QB, E), "z", 0, 0, tiled=True)
    query_grad = jnp.sum(u_in, axis=0)
    cand_grad = (pieces[0] + pieces[1]) + (pieces[2] + pieces[3])
    return query_grad, cand_grad


def solution(mesh):
    fine = Mesh(mesh.devices.reshape(2, 2, 2, 4, 8), AXES)
    split = P(AXES)
    in_specs = (P(AXES, None), P(AXES, None), split, split, split, P())
    out_specs = (P(AXES, None), P(AXES, None))
    return jax.shard_map(
        per_device, mesh=fine, in_specs=in_specs, out_specs=out_specs, check_vma=False
    )
```

```python
import functools

import jax
import jax.numpy as jnp
from jax import lax
from jax.experimental import pallas as pl
from jax.experimental.pallas import tpu as pltpu
from jax.sharding import Mesh, PartitionSpec as P

bf16 = jnp.bfloat16
f32 = jnp.float32
i32 = jnp.int32
NT = (((1,), (1,)), ((), ()))
NN = (((1,), (0,)), ((), ()))
TN = (((0,), (0,)), ((), ()))
AXES = ("yl", "c", "yh", "x", "z")
GROUP = ("x", "z")
RING = ("yl", "yh")
NY, NX, NZ, NCORE = 4, 4, 8, 2
NGROUP = NX * NZ
VMEM = pl.BlockSpec(memory_space=pltpu.VMEM)
SMEM = pl.BlockSpec(memory_space=pltpu.SMEM)
E = 128
QB = 64
CB = 512
QPAD = 8
CPAD = 16
SIDE = 32
NQ = NGROUP * QB
HALF = NY * CB
QUART = NZ * QB
NC = NCORE * HALF


def pack_kernel(queries, positive, weight, candidates, bucket, q_out, c_out):
    place = positive[...]
    rows = [
        weight[...].astype(f32),
        (place >> 12).astype(f32),
        ((place >> 6) & 63).astype(f32),
        (place & 63).astype(f32),
        jnp.zeros((QPAD - 4, QB), f32),
    ]
    notes = jnp.concatenate(rows, axis=0)
    notes = jnp.concatenate([notes, notes], axis=1).astype(bf16)
    block = queries[...]
    for k in range(NGROUP):
        q_out[k, :QB, :] = block
        q_out[k, QB:, :] = notes
    codes = bucket[...]
    c_out[:CB, :] = candidates[...]
    c_out[CB:, :] = jnp.concatenate(
        [(codes >> 5).astype(f32), (codes & 31).astype(f32), jnp.zeros((CPAD - 8, E), f32)], axis=0
    ).astype(bf16)


def stats_kernel(here, table, q_in, own, other, c_ext, q_ext, aux, lse_out, meta, ref_max, sums):
    lane = lax.broadcasted_iota(i32, (SIDE, E), 1)
    row = lax.broadcasted_iota(i32, (SIDE, E), 0)
    freq = table[...]
    high = freq.astype(bf16).astype(f32)
    rest = freq - high
    middle = rest.astype(bf16).astype(f32)
    low = rest - middle
    parts = jnp.where(
        lane < SIDE, high, jnp.where(lane < 2 * SIDE, middle, jnp.where(lane < 3 * SIDE, low, 0.0))
    ).astype(bf16)
    pick = ((lane & (SIDE - 1)) == row).astype(f32).astype(bf16)

    for core, block_ref in enumerate((own, other)):
        for s in range(NY):
            first = core * HALF + s * CB
            c_ext[first : first + CB, :E] = block_ref[s, :CB, :]
            codes = block_ref[s, CB : CB + CPAD, :].astype(f32)
            for r in range(CB // E):
                major = codes[r : r + 1, :].astype(i32)
                minor = codes[4 + r : 5 + r, :].astype(i32)
                hot_major = (row == major).astype(f32).astype(bf16)
                hot_minor = (row == minor).astype(f32).astype(bf16)
                values = lax.dot_general(hot_major, parts, TN, preferred_element_type=f32)
                mask = lax.dot_general(hot_minor, pick, TN, preferred_element_type=f32)
                c_ext[first + r * E : first + (r + 1) * E, E:] = (-(values * mask)).astype(bf16)

    wide = lax.broadcasted_iota(i32, (8, E), 1)
    q_ext[:, E:] = jnp.ones((NQ, E), bf16)
    for k in range(NGROUP):
        q_ext[k * QB : (k + 1) * QB, :E] = q_in[k, :QB, :]
    for t in range(NGROUP // 2):
        even = q_in[2 * t, QB : QB + QPAD, :].astype(f32)
        odd = q_in[2 * t + 1, QB : QB + QPAD, :].astype(f32)
        meta[:, t * E : (t + 1) * E] = jnp.where(wide < QB, even, odd)
    weight = meta[0:1, :]
    position = (meta[1:2, :] * 4096.0 + meta[2:3, :] * 64.0 + meta[3:4, :]).astype(i32)
    block = position >> 9
    y_there = ((block >> 5) & 1) * 2 + ((block >> 7) & 1)
    c_there = (block >> 6) & 1
    slot = (c_there ^ here[1]) * NY + ((here[0] - y_there) & 3)
    local = jnp.where((block & 31) == here[2], slot * CB + (position & (CB - 1)), -1)
    aux[2:3, :] = weight
    aux[3:4, :] = local.astype(f32)

    rows = 512
    queries = q_ext[...]

    def tall(k):
        start = k * rows if isinstance(k, int) else pl.multiple_of(k * rows, rows)
        logits = lax.dot_general(c_ext[pl.ds(start, rows), :], queries, NT, preferred_element_type=f32)
        return logits.reshape(rows // 8, 8, NQ)

    def summed(logits, shift):
        return jnp.sum(jnp.exp(logits - shift[None]), axis=0)

    block = tall(0)
    first = jnp.max(block, axis=0)
    top, total = first, summed(block, first)
    ref_max[...] = first
    for k in range(1, NC // rows):
        block = tall(k)
        top = jnp.maximum(top, jnp.max(block, axis=0))
        total = total + summed(block, ref_max[...])
    sums[...] = total
    best = jnp.max(top, axis=0, keepdims=True)

    @pl.when(jnp.max(top - ref_max[...]) > 40.0)
    def _():
        peak = jnp.broadcast_to(best, (8, NQ))
        ref_max[...] = peak
        sums[...] = lax.fori_loop(
            0, NC // rows, lambda k, acc: acc + summed(tall(k), peak), jnp.zeros((8, NQ), f32)
        )

    total = jnp.sum(sums[...] * jnp.exp(ref_max[...] - best), axis=0, keepdims=True)
    aux[0:1, :] = best
    aux[1:2, :] = total
    aux[4:8, :] = jnp.zeros((4, NQ), f32)
    lse = best + jnp.log(total)
    tile = jnp.concatenate([lse[:, t * E : (t + 1) * E] for t in range(NQ // E)], axis=0)
    for k in range(NGROUP):
        lse_out[k] = tile


def row_scale(here, aux, lse_all, first, count):
    best = aux[0:1, pl.ds(first, count)]
    tiles = count // E
    if count == NQ:
        theirs = lse_all[...]
    else:
        theirs = jnp.concatenate(
            [lse_all[k, pl.ds(first // E, tiles), :][None] for k in range(NGROUP)], axis=0
        )
    mine = jnp.concatenate([best[:, t * E : (t + 1) * E] for t in range(tiles)], axis=0)
    member = lax.broadcasted_iota(i32, (NGROUP, tiles, E), 0)
    others = jnp.sum(jnp.where(member == here[2], 0.0, jnp.exp(theirs - mine[None])), axis=0)
    others = jnp.concatenate([others[t : t + 1, :] for t in range(tiles)], axis=1)
    weight = aux[2:3, pl.ds(first, count)]
    return weight / (aux[1:2, pl.ds(first, count)] + others)


def grad_kernel(shift, halves, here, c_ext, q_ext, aux, lse_all, *refs):
    n = len(halves)
    before = refs[: len(refs) - 1 - n]
    u_out, g_outs = refs[-1 - n], refs[-n:]
    u_in = before[0] if len(before) in (1, n + 1) and shift == 0 and halves == (0,) else None
    g_ins = before[-n:] if len(before) >= n and shift != 2 else [None] * n
    first = pl.multiple_of(((here[2] >> 3) - shift & 3) * QUART, QUART)
    span = pl.ds(first, QUART)
    scale = row_scale(here, aux, lse_all, first, QUART)
    queries = q_ext[span, :]
    narrow = queries[:, :E]
    best, weight = aux[0:1, span], aux[2:3, span]
    local = aux[3:4, span].astype(i32)
    total = jnp.zeros((QUART, E), f32) if u_in is None else u_in[...]
    for half, g_in, g_out in zip(halves, g_ins, g_outs):
        for k in range(NY):
            row = half * HALF + k * CB
            block = c_ext[row : row + CB, :]
            logits = lax.dot_general(block, queries, NT, preferred_element_type=f32)
            expo = jnp.exp(logits - best) * scale
            matched = lax.broadcasted_iota(i32, logits.shape, 0) == (local - row)
            grad = (expo - jnp.where(matched, weight, 0.0)).astype(bf16)
            g_part = lax.dot_general(grad, narrow, NN, preferred_element_type=f32)
            g_out[k] = g_part if g_in is None else g_in[k] + g_part
            total = total + lax.dot_general(grad, block[:, :E], TN, preferred_element_type=f32)
    u_out[...] = total


def merge_kernel(own, came, *outs):
    for s, out in enumerate(outs):
        out[...] = own[s] + came[s]


def ring(step):
    place = [(y & 1) * 2 + (y >> 1) for y in range(NY)]
    return [(place[y], place[(y + step) % NY]) for y in range(NY)]


def shaped(shape, dtype):
    return jax.ShapeDtypeStruct(shape, dtype)


def cost(pairs, products):
    return pl.CostEstimate(
        flops=pairs * E * products // 2, bytes_accessed=pairs, transcendentals=pairs // 8
    )


PARAMS = pltpu.CompilerParams(vmem_limit_bytes=48 * 2**20)


def per_device(queries, candidates, positive, bucket, query_weight, log_freq):
    y = lax.axis_index("yh") * 2 + lax.axis_index("yl")
    here = jnp.stack([y, lax.axis_index("c"), lax.axis_index(GROUP)]).astype(i32)

    q_block, c_block = pl.pallas_call(
        pack_kernel,
        out_shape=[shaped((NGROUP, QB + QPAD, E), bf16), shaped((CB + CPAD, E), bf16)],
        in_specs=[VMEM] * 5,
        out_specs=[VMEM] * 2,
        compiler_params=pltpu.CompilerParams(vmem_limit_bytes=60 * 2**20),
        name="pack",
    )(
        queries,
        positive.reshape(1, QB),
        query_weight.reshape(1, QB),
        candidates,
        bucket.reshape(4, E),
    )
    q_in = lax.all_to_all(q_block, GROUP, 0, 0, tiled=True)
    spread = [c_block]
    for s in range(1, NY):
        spread.append(lax.ppermute(c_block, RING, ring(s)))
    own = jnp.stack(spread)
    swap = [(0, 1), (1, 0)]
    other = lax.ppermute(own, "c", swap)

    table = jnp.tile(log_freq.reshape(SIDE, SIDE), (1, 4))

    c_ext, q_ext, aux, lse = pl.pallas_call(
        stats_kernel,
        out_shape=[
            shaped((NC, 2 * E), bf16),
            shaped((NQ, 2 * E), bf16),
            shaped((8, NQ), f32),
            shaped((NGROUP, NQ // E, E), f32),
        ],
        in_specs=[SMEM] + [VMEM] * 4,
        out_specs=[VMEM] * 4,
        scratch_shapes=[pltpu.VMEM((8, NQ), f32)] * 3,
        compiler_params=PARAMS,
        cost_estimate=cost(NQ * NC, 1),
        name="stats",
    )(here, table, q_in, own, other)
    lse_all = lax.all_to_all(lse, GROUP, 0, 0, tiled=True)

    def grads(shift, halves, *extra, aliases):
        n = len(halves)
        return pl.pallas_call(
            functools.partial(grad_kernel, shift, halves),
            out_shape=[shaped((QUART, E), f32)] + [shaped((NY, CB, E), f32)] * n,
            in_specs=[SMEM] + [VMEM] * (4 + len(extra)),
            out_specs=[VMEM] * (1 + n),
            input_output_aliases=aliases,
            compiler_params=PARAMS,
            cost_estimate=cost(QUART * HALF * n, 3),
            name="grad",
        )(here, c_ext, q_ext, aux, lse_all, *extra)

    def along_x(piece, shift):
        return lax.ppermute(piece, "x", [(i, (i - shift) % NX) for i in range(NX)])

    piece, g_a, g_b = grads(2, (0, 1), aliases={})
    u_two = along_x(piece, 2)
    piece, g_a, g_b = grads(1, (0, 1), g_a, g_b, aliases={5: 1, 6: 2})
    u_one = along_x(piece, 1)
    piece, g_a, g_b = grads(3, (0, 1), g_a, g_b, aliases={5: 1, 6: 2})
    u_three = along_x(piece, 3)
    u_two, g_b = lax.optimization_barrier((u_two, g_b))
    u_own, g_other = grads(0, (1,), g_b, aliases={5: 1})
    u_one, g_other = lax.optimization_barrier((u_one, g_other))
    g_came = lax.ppermute(g_other, "c", swap)
    u_own, g_own = grads(0, (0,), u_own, g_a, aliases={5: 0, 6: 1})

    pieces = pl.pallas_call(
        merge_kernel,
        out_shape=[shaped((CB, E), f32)] * NY,
        in_specs=[VMEM] * 2,
        out_specs=[VMEM] * NY,
        compiler_params=PARAMS,
        name="merge",
    )(g_own, g_came)
    u_sum = [u_two, u_one, u_three, u_own]
    u_sum[3], *pieces = lax.optimization_barrier((u_sum[3], *pieces))
    for s in range(1, NY):
        pieces[s] = lax.ppermute(pieces[s], RING, ring(-s))
    u_line = (u_sum[0] + u_sum[1]) + (u_sum[2] + u_sum[3])
    u_in = lax.all_to_all(u_line.reshape(NZ, QB, E), "z", 0, 0, tiled=True)
    query_grad = jnp.sum(u_in, axis=0)
    cand_grad = (pieces[0] + pieces[1]) + (pieces[2] + pieces[3])
    return query_grad, cand_grad


def solution(mesh):
    fine = Mesh(mesh.devices.reshape(2, 2, 2, 4, 8), AXES)
    split = P(AXES)
    in_specs = (P(AXES, None), P(AXES, None), split, split, split, P())
    out_specs = (P(AXES, None), P(AXES, None))
    return jax.shard_map(
        per_device, mesh=fine, in_specs=in_specs, out_specs=out_specs, check_vma=False
    )
```

```python
import functools

import jax
import jax.numpy as jnp
from jax import lax
from jax.experimental import pallas as pl
from jax.experimental.pallas import tpu as pltpu
from jax.sharding import Mesh, PartitionSpec as P

bf16 = jnp.bfloat16
f32 = jnp.float32
i32 = jnp.int32
NT = (((1,), (1,)), ((), ()))
NN = (((1,), (0,)), ((), ()))
TN = (((0,), (0,)), ((), ()))
AXES = ("yl", "c", "yh", "x", "z")
GROUP = ("x", "z")
RING = ("yl", "yh")
NY, NX, NZ, NCORE = 4, 4, 8, 2
NGROUP = NX * NZ
VMEM = pl.BlockSpec(memory_space=pltpu.VMEM)
SMEM = pl.BlockSpec(memory_space=pltpu.SMEM)
E = 128
QB = 64
CB = 512
QPAD = 8
CPAD = 16
SIDE = 32
NQ = NGROUP * QB
HALF = NY * CB
QUART = NZ * QB
KEPT = 7
NC = NCORE * HALF


def pack_kernel(queries, positive, weight, candidates, bucket, q_out, c_out):
    place = positive[...]
    rows = [
        weight[...].astype(f32),
        (place >> 12).astype(f32),
        ((place >> 6) & 63).astype(f32),
        (place & 63).astype(f32),
        jnp.zeros((QPAD - 4, QB), f32),
    ]
    notes = jnp.concatenate(rows, axis=0)
    notes = jnp.concatenate([notes, notes], axis=1).astype(bf16)
    block = queries[...]
    for k in range(NGROUP):
        q_out[k, :QB, :] = block
        q_out[k, QB:, :] = notes
    codes = bucket[...]
    c_out[:CB, :] = candidates[...]
    c_out[CB:, :] = jnp.concatenate(
        [(codes >> 5).astype(f32), (codes & 31).astype(f32), jnp.zeros((CPAD - 8, E), f32)], axis=0
    ).astype(bf16)


def stats_kernel(here, table, q_in, own, other, c_ext, q_ext, aux, lse_out, *refs):
    kept, (meta, ref_max, sums) = refs[:KEPT], refs[KEPT:]
    lane = lax.broadcasted_iota(i32, (SIDE, E), 1)
    row = lax.broadcasted_iota(i32, (SIDE, E), 0)
    freq = table[...]
    high = freq.astype(bf16).astype(f32)
    rest = freq - high
    middle = rest.astype(bf16).astype(f32)
    low = rest - middle
    parts = jnp.where(
        lane < SIDE, high, jnp.where(lane < 2 * SIDE, middle, jnp.where(lane < 3 * SIDE, low, 0.0))
    ).astype(bf16)
    pick = ((lane & (SIDE - 1)) == row).astype(f32).astype(bf16)

    for core, block_ref in enumerate((own, other)):
        for s in range(NY):
            first = core * HALF + s * CB
            c_ext[first : first + CB, :E] = block_ref[s, :CB, :]
            codes = block_ref[s, CB : CB + CPAD, :].astype(f32)
            for r in range(CB // E):
                major = codes[r : r + 1, :].astype(i32)
                minor = codes[4 + r : 5 + r, :].astype(i32)
                hot_major = (row == major).astype(f32).astype(bf16)
                hot_minor = (row == minor).astype(f32).astype(bf16)
                values = lax.dot_general(hot_major, parts, TN, preferred_element_type=f32)
                mask = lax.dot_general(hot_minor, pick, TN, preferred_element_type=f32)
                c_ext[first + r * E : first + (r + 1) * E, E:] = (-(values * mask)).astype(bf16)

    wide = lax.broadcasted_iota(i32, (8, E), 1)
    q_ext[:, E:] = jnp.ones((NQ, E), bf16)
    for k in range(NGROUP):
        q_ext[k * QB : (k + 1) * QB, :E] = q_in[k, :QB, :]
    for t in range(NGROUP // 2):
        even = q_in[2 * t, QB : QB + QPAD, :].astype(f32)
        odd = q_in[2 * t + 1, QB : QB + QPAD, :].astype(f32)
        meta[:, t * E : (t + 1) * E] = jnp.where(wide < QB, even, odd)
    weight = meta[0:1, :]
    position = (meta[1:2, :] * 4096.0 + meta[2:3, :] * 64.0 + meta[3:4, :]).astype(i32)
    block = position >> 9
    y_there = ((block >> 5) & 1) * 2 + ((block >> 7) & 1)
    c_there = (block >> 6) & 1
    slot = (c_there ^ here[1]) * NY + ((here[0] - y_there) & 3)
    local = jnp.where((block & 31) == here[2], slot * CB + (position & (CB - 1)), -1)
    aux[2:3, :] = weight
    aux[3:4, :] = local.astype(f32)

    rows = 512
    queries = q_ext[...]

    def tall(k):
        start = k * rows if isinstance(k, int) else pl.multiple_of(k * rows, rows)
        logits = lax.dot_general(c_ext[pl.ds(start, rows), :], queries, NT, preferred_element_type=f32)
        if isinstance(k, int) and k < KEPT:
            kept[k][...] = logits
        return logits.reshape(rows // 8, 8, NQ)

    def summed(logits, shift):
        return jnp.sum(jnp.exp(logits - shift[None]), axis=0)

    block = tall(0)
    first = jnp.max(block, axis=0)
    top, total = first, summed(block, first)
    ref_max[...] = first
    for k in range(1, NC // rows):
        block = tall(k)
        top = jnp.maximum(top, jnp.max(block, axis=0))
        total = total + summed(block, ref_max[...])
    sums[...] = total
    best = jnp.max(top, axis=0, keepdims=True)

    @pl.when(jnp.max(top - ref_max[...]) > 40.0)
    def _():
        peak = jnp.broadcast_to(best, (8, NQ))
        ref_max[...] = peak
        sums[...] = lax.fori_loop(
            0, NC // rows, lambda k, acc: acc + summed(tall(k), peak), jnp.zeros((8, NQ), f32)
        )

    total = jnp.sum(sums[...] * jnp.exp(ref_max[...] - best), axis=0, keepdims=True)
    aux[0:1, :] = best
    aux[1:2, :] = total
    aux[4:8, :] = jnp.zeros((4, NQ), f32)
    lse = best + jnp.log(total)
    tile = jnp.concatenate([lse[:, t * E : (t + 1) * E] for t in range(NQ // E)], axis=0)
    for k in range(NGROUP):
        lse_out[k] = tile


def row_scale(here, aux, lse_all, first, count):
    best = aux[0:1, pl.ds(first, count)]
    tiles = count // E
    if count == NQ:
        theirs = lse_all[...]
    else:
        theirs = jnp.concatenate(
            [lse_all[k, pl.ds(first // E, tiles), :][None] for k in range(NGROUP)], axis=0
        )
    mine = jnp.concatenate([best[:, t * E : (t + 1) * E] for t in range(tiles)], axis=0)
    member = lax.broadcasted_iota(i32, (NGROUP, tiles, E), 0)
    others = jnp.sum(jnp.where(member == here[2], 0.0, jnp.exp(theirs - mine[None])), axis=0)
    others = jnp.concatenate([others[t : t + 1, :] for t in range(tiles)], axis=1)
    weight = aux[2:3, pl.ds(first, count)]
    return weight / (aux[1:2, pl.ds(first, count)] + others)


def grad_kernel(shift, halves, here, c_ext, q_ext, aux, lse_all, *refs):
    n = len(halves)
    kept, refs = refs[: KEPT], refs[KEPT:]
    before = refs[: len(refs) - 1 - n]
    u_out, g_outs = refs[-1 - n], refs[-n:]
    u_in = before[0] if len(before) in (1, n + 1) and shift == 0 and halves == (0,) else None
    g_ins = before[-n:] if len(before) >= n and shift != 2 else [None] * n
    first = pl.multiple_of(((here[2] >> 3) - shift & 3) * QUART, QUART)
    span = pl.ds(first, QUART)
    scale = row_scale(here, aux, lse_all, first, QUART)
    queries = q_ext[span, :]
    narrow = queries[:, :E]
    best, weight = aux[0:1, span], aux[2:3, span]
    local = aux[3:4, span].astype(i32)
    total = jnp.zeros((QUART, E), f32) if u_in is None else u_in[...]
    for half, g_in, g_out in zip(halves, g_ins, g_outs):
        for k in range(NY):
            row = half * HALF + k * CB
            block = c_ext[row : row + CB, :]
            if half * NY + k < KEPT:
                logits = kept[half * NY + k][:, span]
            else:
                logits = lax.dot_general(block, queries, NT, preferred_element_type=f32)
            expo = jnp.exp(logits - best) * scale
            matched = lax.broadcasted_iota(i32, logits.shape, 0) == (local - row)
            grad = (expo - jnp.where(matched, weight, 0.0)).astype(bf16)
            g_part = lax.dot_general(grad, narrow, NN, preferred_element_type=f32)
            g_out[k] = g_part if g_in is None else g_in[k] + g_part
            total = total + lax.dot_general(grad, block[:, :E], TN, preferred_element_type=f32)
    u_out[...] = total


def merge_kernel(own, came, *outs):
    for s, out in enumerate(outs):
        out[...] = own[s] + came[s]


def ring(step):
    place = [(y & 1) * 2 + (y >> 1) for y in range(NY)]
    return [(place[y], place[(y + step) % NY]) for y in range(NY)]


def shaped(shape, dtype):
    return jax.ShapeDtypeStruct(shape, dtype)


def cost(pairs, products):
    return pl.CostEstimate(
        flops=pairs * E * products // 2, bytes_accessed=pairs, transcendentals=pairs // 8
    )


PARAMS = pltpu.CompilerParams(vmem_limit_bytes=18 * 2**20)


def per_device(queries, candidates, positive, bucket, query_weight, log_freq):
    y = lax.axis_index("yh") * 2 + lax.axis_index("yl")
    here = jnp.stack([y, lax.axis_index("c"), lax.axis_index(GROUP)]).astype(i32)

    q_block, c_block = pl.pallas_call(
        pack_kernel,
        out_shape=[shaped((NGROUP, QB + QPAD, E), bf16), shaped((CB + CPAD, E), bf16)],
        in_specs=[VMEM] * 5,
        out_specs=[VMEM] * 2,
        compiler_params=pltpu.CompilerParams(vmem_limit_bytes=60 * 2**20),
        name="pack",
    )(
        queries,
        positive.reshape(1, QB),
        query_weight.reshape(1, QB),
        candidates,
        bucket.reshape(4, E),
    )
    q_in = lax.all_to_all(q_block, GROUP, 0, 0, tiled=True)
    spread = [c_block]
    for s in range(1, NY):
        spread.append(lax.ppermute(c_block, RING, ring(s)))
    own = jnp.stack(spread)
    swap = [(0, 1), (1, 0)]
    other = lax.ppermute(own, "c", swap)

    table = jnp.tile(log_freq.reshape(SIDE, SIDE), (1, 4))

    c_ext, q_ext, aux, lse, *kept = pl.pallas_call(
        stats_kernel,
        out_shape=[
            shaped((NC, 2 * E), bf16),
            shaped((NQ, 2 * E), bf16),
            shaped((8, NQ), f32),
            shaped((NGROUP, NQ // E, E), f32),
        ]
        + [shaped((CB, NQ), f32)] * KEPT,
        in_specs=[SMEM] + [VMEM] * 4,
        out_specs=[VMEM] * (4 + KEPT),
        scratch_shapes=[pltpu.VMEM((8, NQ), f32)] * 3,
        compiler_params=PARAMS,
        cost_estimate=cost(NQ * NC, 1),
        name="stats",
    )(here, table, q_in, own, other)
    lse_all = lax.all_to_all(lse, GROUP, 0, 0, tiled=True)

    def grads(shift, halves, *extra, aliases):
        n = len(halves)
        return pl.pallas_call(
            functools.partial(grad_kernel, shift, halves),
            out_shape=[shaped((QUART, E), f32)] + [shaped((NY, CB, E), f32)] * n,
            in_specs=[SMEM] + [VMEM] * (4 + KEPT + len(extra)),
            out_specs=[VMEM] * (1 + n),
            input_output_aliases={i + KEPT: o for i, o in aliases.items()},
            compiler_params=PARAMS,
            cost_estimate=cost(QUART * HALF * n, 3),
            name="grad",
        )(here, c_ext, q_ext, aux, lse_all, *kept, *extra)

    def along_x(piece, shift):
        return lax.ppermute(piece, "x", [(i, (i - shift) % NX) for i in range(NX)])

    piece, g_a, g_b = grads(2, (0, 1), aliases={})
    u_two = along_x(piece, 2)
    piece, g_a, g_b = grads(1, (0, 1), g_a, g_b, aliases={5: 1, 6: 2})
    u_one = along_x(piece, 1)
    piece, g_a, g_b = grads(3, (0, 1), g_a, g_b, aliases={5: 1, 6: 2})
    u_three = along_x(piece, 3)
    u_two, g_b = lax.optimization_barrier((u_two, g_b))
    u_own, g_other = grads(0, (1,), g_b, aliases={5: 1})
    u_one, g_other = lax.optimization_barrier((u_one, g_other))
    g_came = lax.ppermute(g_other, "c", swap)
    u_own, g_own = grads(0, (0,), u_own, g_a, aliases={5: 0, 6: 1})

    pieces = pl.pallas_call(
        merge_kernel,
        out_shape=[shaped((CB, E), f32)] * NY,
        in_specs=[VMEM] * 2,
        out_specs=[VMEM] * NY,
        compiler_params=PARAMS,
        name="merge",
    )(g_own, g_came)
    u_sum = [u_two, u_one, u_three, u_own]
    u_sum[3], *pieces = lax.optimization_barrier((u_sum[3], *pieces))
    for s in range(1, NY):
        pieces[s] = lax.ppermute(pieces[s], RING, ring(-s))
    u_line = (u_sum[0] + u_sum[1]) + (u_sum[2] + u_sum[3])
    u_in = lax.all_to_all(u_line.reshape(NZ, QB, E), "z", 0, 0, tiled=True)
    query_grad = jnp.sum(u_in, axis=0)
    cand_grad = (pieces[0] + pieces[1]) + (pieces[2] + pieces[3])
    return query_grad, cand_grad


def solution(mesh):
    fine = Mesh(mesh.devices.reshape(2, 2, 2, 4, 8), AXES)
    split = P(AXES)
    in_specs = (P(AXES, None), P(AXES, None), split, split, split, P())
    out_specs = (P(AXES, None), P(AXES, None))
    return jax.shard_map(
        per_device, mesh=fine, in_specs=in_specs, out_specs=out_specs, check_vma=False
    )
```

```python
import functools

import jax
import jax.numpy as jnp
from jax import lax
from jax.experimental import pallas as pl
from jax.experimental.pallas import tpu as pltpu
from jax.sharding import Mesh, PartitionSpec as P

bf16 = jnp.bfloat16
f32 = jnp.float32
i32 = jnp.int32
NT = (((1,), (1,)), ((), ()))
NN = (((1,), (0,)), ((), ()))
TN = (((0,), (0,)), ((), ()))
AXES = ("yl", "c", "yh", "x", "z")
GROUP = ("x", "z")
RING = ("yl", "yh")
NY, NX, NZ, NCORE = 4, 4, 8, 2
NGROUP = NX * NZ
VMEM = pl.BlockSpec(memory_space=pltpu.VMEM)
SMEM = pl.BlockSpec(memory_space=pltpu.SMEM)
E = 128
QB = 64
CB = 512
QPAD = 8
CPAD = 16
SIDE = 32
NQ = NGROUP * QB
HALF = NY * CB
QUART = NZ * QB
KEPT = 7
NC = NCORE * HALF


def pack_kernel(queries, positive, weight, candidates, bucket, q_out, c_out):
    place = positive[...]
    rows = [
        weight[...].astype(f32),
        (place >> 12).astype(f32),
        ((place >> 6) & 63).astype(f32),
        (place & 63).astype(f32),
        jnp.zeros((QPAD - 4, QB), f32),
    ]
    notes = jnp.concatenate(rows, axis=0)
    notes = jnp.concatenate([notes, notes], axis=1).astype(bf16)
    block = queries[...]
    for k in range(NGROUP):
        q_out[k, :QB, :] = block
        q_out[k, QB:, :] = notes
    codes = bucket[...]
    c_out[:CB, :] = candidates[...]
    c_out[CB:, :] = jnp.concatenate(
        [(codes >> 5).astype(f32), (codes & 31).astype(f32), jnp.zeros((CPAD - 8, E), f32)], axis=0
    ).astype(bf16)


def stats_kernel(here, table, q_in, own, other, c_ext, q_ext, aux, lse_out, *refs):
    kept, (meta, ref_max, sums) = refs[:KEPT], refs[KEPT:]
    lane = lax.broadcasted_iota(i32, (SIDE, E), 1)
    row = lax.broadcasted_iota(i32, (SIDE, E), 0)
    freq = table[...]
    high = freq.astype(bf16).astype(f32)
    rest = freq - high
    middle = rest.astype(bf16).astype(f32)
    low = rest - middle
    parts = jnp.where(
        lane < SIDE, high, jnp.where(lane < 2 * SIDE, middle, jnp.where(lane < 3 * SIDE, low, 0.0))
    ).astype(bf16)
    pick = ((lane & (SIDE - 1)) == row).astype(f32).astype(bf16)

    for core, block_ref in enumerate((own, other)):
        for s in range(NY):
            first = core * HALF + s * CB
            c_ext[first : first + CB, :E] = block_ref[s, :CB, :]
            codes = block_ref[s, CB : CB + CPAD, :].astype(f32)
            for r in range(CB // E):
                major = codes[r : r + 1, :].astype(i32)
                minor = codes[4 + r : 5 + r, :].astype(i32)
                hot_major = (row == major).astype(f32).astype(bf16)
                hot_minor = (row == minor).astype(f32).astype(bf16)
                values = lax.dot_general(hot_major, parts, TN, preferred_element_type=f32)
                mask = lax.dot_general(hot_minor, pick, TN, preferred_element_type=f32)
                c_ext[first + r * E : first + (r + 1) * E, E:] = (-(values * mask)).astype(bf16)

    wide = lax.broadcasted_iota(i32, (8, E), 1)
    q_ext[:, E:] = jnp.ones((NQ, E), bf16)
    for k in range(NGROUP):
        q_ext[k * QB : (k + 1) * QB, :E] = q_in[k, :QB, :]
    for t in range(NGROUP // 2):
        even = q_in[2 * t, QB : QB + QPAD, :].astype(f32)
        odd = q_in[2 * t + 1, QB : QB + QPAD, :].astype(f32)
        meta[:, t * E : (t + 1) * E] = jnp.where(wide < QB, even, odd)
    weight = meta[0:1, :]
    position = (meta[1:2, :] * 4096.0 + meta[2:3, :] * 64.0 + meta[3:4, :]).astype(i32)
    block = position >> 9
    y_there = ((block >> 5) & 1) * 2 + ((block >> 7) & 1)
    c_there = (block >> 6) & 1
    slot = (c_there ^ here[1]) * NY + ((here[0] - y_there) & 3)
    local = jnp.where((block & 31) == here[2], slot * CB + (position & (CB - 1)), -1)
    aux[2:3, :] = weight
    aux[3:4, :] = local.astype(f32)

    rows = 512
    queries = q_ext[...]

    def tall(k):
        start = k * rows if isinstance(k, int) else pl.multiple_of(k * rows, rows)
        logits = lax.dot_general(c_ext[pl.ds(start, rows), :], queries, NT, preferred_element_type=f32)
        if isinstance(k, int) and k < KEPT:
            kept[k][...] = logits
        return logits.reshape(rows // 8, 8, NQ)

    def summed(logits, shift):
        return jnp.sum(jnp.exp(logits - shift[None]), axis=0)

    block = tall(0)
    first = jnp.max(block, axis=0)
    top, total = first, summed(block, first)
    ref_max[...] = first
    for k in range(1, NC // rows):
        block = tall(k)
        top = jnp.maximum(top, jnp.max(block, axis=0))
        total = total + summed(block, ref_max[...])
    sums[...] = total
    best = jnp.max(top, axis=0, keepdims=True)

    @pl.when(jnp.max(top - ref_max[...]) > 40.0)
    def _():
        peak = jnp.broadcast_to(best, (8, NQ))
        ref_max[...] = peak
        sums[...] = lax.fori_loop(
            0, NC // rows, lambda k, acc: acc + summed(tall(k), peak), jnp.zeros((8, NQ), f32)
        )

    total = jnp.sum(sums[...] * jnp.exp(ref_max[...] - best), axis=0, keepdims=True)
    aux[0:1, :] = best
    aux[1:2, :] = total
    aux[4:8, :] = jnp.zeros((4, NQ), f32)
    lse = best + jnp.log(total)
    tile = jnp.concatenate([lse[:, t * E : (t + 1) * E] for t in range(NQ // E)], axis=0)
    for k in range(NGROUP):
        lse_out[k] = tile


def row_scale(here, aux, lse_all, first, count):
    best = aux[0:1, pl.ds(first, count)]
    tiles = count // E
    if count == NQ:
        theirs = lse_all[...]
    else:
        theirs = jnp.concatenate(
            [lse_all[k, pl.ds(first // E, tiles), :][None] for k in range(NGROUP)], axis=0
        )
    mine = jnp.concatenate([best[:, t * E : (t + 1) * E] for t in range(tiles)], axis=0)
    member = lax.broadcasted_iota(i32, (NGROUP, tiles, E), 0)
    others = jnp.sum(jnp.where(member == here[2], 0.0, jnp.exp(theirs - mine[None])), axis=0)
    others = jnp.concatenate([others[t : t + 1, :] for t in range(tiles)], axis=1)
    weight = aux[2:3, pl.ds(first, count)]
    return weight / (aux[1:2, pl.ds(first, count)] + others)


def grad_kernel(shift, halves, here, c_ext, q_ext, aux, lse_all, *refs):
    n = len(halves)
    kept, refs = refs[: KEPT], refs[KEPT:]
    before = refs[: len(refs) - 1 - n]
    u_out, g_outs = refs[-1 - n], refs[-n:]
    u_in = before[0] if len(before) in (1, n + 1) and shift == 0 and halves == (0,) else None
    g_ins = before[-n:] if len(before) >= n and shift != 2 else [None] * n
    first = pl.multiple_of(((here[2] >> 3) - shift & 3) * QUART, QUART)
    span = pl.ds(first, QUART)
    scale = row_scale(here, aux, lse_all, first, QUART)
    queries = q_ext[span, :]
    narrow = queries[:, :E]
    best, weight = aux[0:1, span], aux[2:3, span]
    local = aux[3:4, span].astype(i32)
    total = jnp.zeros((QUART, E), f32) if u_in is None else u_in[...]
    for half, g_in, g_out in zip(halves, g_ins, g_outs):
        for k in range(NY):
            row = half * HALF + k * CB
            block = c_ext[row : row + CB, :]
            if half * NY + k < KEPT:
                logits = kept[half * NY + k][:, span]
            else:
                logits = lax.dot_general(block, queries, NT, preferred_element_type=f32)
            expo = jnp.exp(logits - best) * scale
            matched = lax.broadcasted_iota(i32, logits.shape, 0) == (local - row)
            grad = (expo - jnp.where(matched, weight, 0.0)).astype(bf16)
            g_part = lax.dot_general(grad, narrow, NN, preferred_element_type=f32)
            g_out[k] = g_part if g_in is None else g_in[k] + g_part
            total = total + lax.dot_general(grad, block[:, :E], TN, preferred_element_type=f32)
    u_out[...] = total


def merge_kernel(own, came, *outs):
    for s, out in enumerate(outs):
        out[...] = own[s] + came[s]


def add_kernel(a, b, c, d, out):
    out[...] = (a[...] + b[...]) + (c[...] + d[...])


def ring(step):
    place = [(y & 1) * 2 + (y >> 1) for y in range(NY)]
    return [(place[y], place[(y + step) % NY]) for y in range(NY)]


def shaped(shape, dtype):
    return jax.ShapeDtypeStruct(shape, dtype)


def cost(pairs, products):
    return pl.CostEstimate(
        flops=pairs * E * products // 2, bytes_accessed=pairs, transcendentals=pairs // 8
    )


PARAMS = pltpu.CompilerParams(vmem_limit_bytes=18 * 2**20)


def per_device(queries, candidates, positive, bucket, query_weight, log_freq):
    y = lax.axis_index("yh") * 2 + lax.axis_index("yl")
    here = jnp.stack([y, lax.axis_index("c"), lax.axis_index(GROUP)]).astype(i32)

    q_block, c_block = pl.pallas_call(
        pack_kernel,
        out_shape=[shaped((NGROUP, QB + QPAD, E), bf16), shaped((CB + CPAD, E), bf16)],
        in_specs=[VMEM] * 5,
        out_specs=[VMEM] * 2,
        compiler_params=pltpu.CompilerParams(vmem_limit_bytes=60 * 2**20),
        name="pack",
    )(
        queries,
        positive.reshape(1, QB),
        query_weight.reshape(1, QB),
        candidates,
        bucket.reshape(4, E),
    )
    q_in = lax.all_to_all(q_block, GROUP, 0, 0, tiled=True)
    spread = [c_block]
    for s in range(1, NY):
        spread.append(lax.ppermute(c_block, RING, ring(s)))
    own = jnp.stack(spread)
    swap = [(0, 1), (1, 0)]
    other = lax.ppermute(own, "c", swap)

    table = jnp.tile(log_freq.reshape(SIDE, SIDE), (1, 4))

    c_ext, q_ext, aux, lse, *kept = pl.pallas_call(
        stats_kernel,
        out_shape=[
            shaped((NC, 2 * E), bf16),
            shaped((NQ, 2 * E), bf16),
            shaped((8, NQ), f32),
            shaped((NGROUP, NQ // E, E), f32),
        ]
        + [shaped((CB, NQ), f32)] * KEPT,
        in_specs=[SMEM] + [VMEM] * 4,
        out_specs=[VMEM] * (4 + KEPT),
        scratch_shapes=[pltpu.VMEM((8, NQ), f32)] * 3,
        compiler_params=PARAMS,
        cost_estimate=cost(NQ * NC, 1),
        name="stats",
    )(here, table, q_in, own, other)
    lse_all = lax.all_to_all(lse, GROUP, 0, 0, tiled=True)

    def grads(shift, halves, *extra, aliases):
        n = len(halves)
        return pl.pallas_call(
            functools.partial(grad_kernel, shift, halves),
            out_shape=[shaped((QUART, E), f32)] + [shaped((NY, CB, E), f32)] * n,
            in_specs=[SMEM] + [VMEM] * (4 + KEPT + len(extra)),
            out_specs=[VMEM] * (1 + n),
            input_output_aliases={i + KEPT: o for i, o in aliases.items()},
            compiler_params=PARAMS,
            cost_estimate=cost(QUART * HALF * n, 3),
            name="grad",
        )(here, c_ext, q_ext, aux, lse_all, *kept, *extra)

    def along_x(piece, shift):
        return lax.ppermute(piece, "x", [(i, (i - shift) % NX) for i in range(NX)])

    piece, g_a, g_b = grads(2, (0, 1), aliases={})
    u_two = along_x(piece, 2)
    piece, g_a, g_b = grads(1, (0, 1), g_a, g_b, aliases={5: 1, 6: 2})
    u_one = along_x(piece, 1)
    piece, g_a, g_b = grads(3, (0, 1), g_a, g_b, aliases={5: 1, 6: 2})
    u_three = along_x(piece, 3)
    u_two, g_b = lax.optimization_barrier((u_two, g_b))
    u_own, g_other = grads(0, (1,), g_b, aliases={5: 1})
    u_one, g_other = lax.optimization_barrier((u_one, g_other))
    g_came = lax.ppermute(g_other, "c", swap)
    u_own, g_own = grads(0, (0,), u_own, g_a, aliases={5: 0, 6: 1})

    u_line = pl.pallas_call(
        add_kernel,
        out_shape=shaped((QUART, E), f32),
        in_specs=[VMEM] * 4,
        out_specs=VMEM,
        compiler_params=PARAMS,
        cost_estimate=cost(NQ * NC, 150),
        name="add",
    )(u_two, u_one, u_three, u_own)
    u_line, g_own = lax.optimization_barrier((u_line, g_own))
    pieces = pl.pallas_call(
        merge_kernel,
        out_shape=[shaped((CB, E), f32)] * NY,
        in_specs=[VMEM] * 2,
        out_specs=[VMEM] * NY,
        compiler_params=PARAMS,
        name="merge",
    )(g_own, g_came)
    u_line, *pieces = lax.optimization_barrier((u_line, *pieces))
    for s in range(1, NY):
        pieces[s] = lax.ppermute(pieces[s], RING, ring(-s))
    u_in = lax.all_to_all(u_line.reshape(NZ, QB, E), "z", 0, 0, tiled=True)
    query_grad = jnp.sum(u_in, axis=0)
    cand_grad = (pieces[0] + pieces[1]) + (pieces[2] + pieces[3])
    return query_grad, cand_grad


def solution(mesh):
    fine = Mesh(mesh.devices.reshape(2, 2, 2, 4, 8), AXES)
    split = P(AXES)
    in_specs = (P(AXES, None), P(AXES, None), split, split, split, P())
    out_specs = (P(AXES, None), P(AXES, None))
    return jax.shard_map(
        per_device, mesh=fine, in_specs=in_specs, out_specs=out_specs, check_vma=False
    )
```

```python
import functools

import jax
import jax.numpy as jnp
from jax import lax
from jax.experimental import pallas as pl
from jax.experimental.pallas import tpu as pltpu
from jax.sharding import Mesh, PartitionSpec as P

bf16 = jnp.bfloat16
f32 = jnp.float32
i32 = jnp.int32
NT = (((1,), (1,)), ((), ()))
NN = (((1,), (0,)), ((), ()))
TN = (((0,), (0,)), ((), ()))
AXES = ("yl", "c", "yh", "x", "z")
GROUP = ("x", "z")
RING = ("yl", "yh")
NY, NX, NZ, NCORE = 4, 4, 8, 2
NGROUP = NX * NZ
VMEM = pl.BlockSpec(memory_space=pltpu.VMEM)
SMEM = pl.BlockSpec(memory_space=pltpu.SMEM)
E = 128
QB = 64
CB = 512
QPAD = 8
CPAD = 16
SIDE = 32
NQ = NGROUP * QB
HALF = NY * CB
QUART = NZ * QB
KEPT = 7
NC = NCORE * HALF


def pack_kernel(queries, positive, weight, candidates, bucket, q_out, c_out):
    place = positive[...]
    rows = [
        weight[...].astype(f32),
        (place >> 12).astype(f32),
        ((place >> 6) & 63).astype(f32),
        (place & 63).astype(f32),
        jnp.zeros((QPAD - 4, QB), f32),
    ]
    notes = jnp.concatenate(rows, axis=0)
    notes = jnp.concatenate([notes, notes], axis=1).astype(bf16)
    block = queries[...]
    for k in range(NGROUP):
        q_out[k, :QB, :] = block
        q_out[k, QB:, :] = notes
    codes = bucket[...]
    c_out[:CB, :] = candidates[...]
    c_out[CB:, :] = jnp.concatenate(
        [(codes >> 5).astype(f32), (codes & 31).astype(f32), jnp.zeros((CPAD - 8, E), f32)], axis=0
    ).astype(bf16)


def stats_kernel(here, table, q_in, own, other, c_ext, q_ext, aux, lse_out, *refs):
    kept, (meta, base_max, sums) = refs[:KEPT], refs[KEPT:]
    lane = lax.broadcasted_iota(i32, (SIDE, E), 1)
    row = lax.broadcasted_iota(i32, (SIDE, E), 0)
    freq = table[...]
    high = freq.astype(bf16).astype(f32)
    rest = freq - high
    middle = rest.astype(bf16).astype(f32)
    low = rest - middle
    parts = jnp.where(
        lane < SIDE, high, jnp.where(lane < 2 * SIDE, middle, jnp.where(lane < 3 * SIDE, low, 0.0))
    ).astype(bf16)
    pick = ((lane & (SIDE - 1)) == row).astype(f32).astype(bf16)

    for core, block_ref in enumerate((own, other)):
        for s in range(NY):
            first = core * HALF + s * CB
            c_ext[first : first + CB, :E] = block_ref[s, :CB, :]
            codes = block_ref[s, CB : CB + CPAD, :].astype(f32)
            for r in range(CB // E):
                major = codes[r : r + 1, :].astype(i32)
                minor = codes[4 + r : 5 + r, :].astype(i32)
                hot_major = (row == major).astype(f32).astype(bf16)
                hot_minor = (row == minor).astype(f32).astype(bf16)
                values = lax.dot_general(hot_major, parts, TN, preferred_element_type=f32)
                mask = lax.dot_general(hot_minor, pick, TN, preferred_element_type=f32)
                c_ext[first + r * E : first + (r + 1) * E, E:] = (-(values * mask)).astype(bf16)

    wide = lax.broadcasted_iota(i32, (8, E), 1)
    q_ext[:, E:] = jnp.ones((NQ, E), bf16)
    for k in range(NGROUP):
        q_ext[k * QB : (k + 1) * QB, :E] = q_in[k, :QB, :]
    for t in range(NGROUP // 2):
        even = q_in[2 * t, QB : QB + QPAD, :].astype(f32)
        odd = q_in[2 * t + 1, QB : QB + QPAD, :].astype(f32)
        meta[:, t * E : (t + 1) * E] = jnp.where(wide < QB, even, odd)
    weight = meta[0:1, :]
    position = (meta[1:2, :] * 4096.0 + meta[2:3, :] * 64.0 + meta[3:4, :]).astype(i32)
    block = position >> 9
    y_there = ((block >> 5) & 1) * 2 + ((block >> 7) & 1)
    c_there = (block >> 6) & 1
    slot = (c_there ^ here[1]) * NY + ((here[0] - y_there) & 3)
    local = jnp.where((block & 31) == here[2], slot * CB + (position & (CB - 1)), -1)
    aux[2:3, :] = weight
    aux[3:4, :] = local.astype(f32)

    rows = 512
    queries = q_ext[...]

    def tall(k):
        logits = lax.dot_general(
            c_ext[k * rows : (k + 1) * rows, :], queries, NT, preferred_element_type=f32
        )
        return logits.reshape(rows // 8, 8, NQ)

    def summed(k, logits):
        expo = jnp.exp(logits - base_max[...][None])
        if k < KEPT:
            kept[k][...] = expo.reshape(rows, NQ)
        return jnp.sum(expo, axis=0)

    block = tall(0)
    top = jnp.max(block, axis=0)
    base_max[...] = jnp.broadcast_to(jnp.max(top, axis=0, keepdims=True), (8, NQ))
    total = summed(0, block)
    for k in range(1, NC // rows):
        block = tall(k)
        top = jnp.maximum(top, jnp.max(block, axis=0))
        total = total + summed(k, block)
    sums[...] = total
    best = jnp.max(top, axis=0, keepdims=True)

    @pl.when(jnp.max(best - base_max[0:1, :]) > 40.0)
    def _():
        base_max[...] = jnp.broadcast_to(best, (8, NQ))
        again = summed(0, tall(0))
        for k in range(1, NC // rows):
            again = again + summed(k, tall(k))
        sums[...] = again

    base = base_max[0:1, :]
    lift = jnp.exp(base - best)
    total = jnp.sum(sums[...], axis=0, keepdims=True) * lift
    aux[0:1, :] = best
    aux[1:2, :] = total
    aux[4:5, :] = base
    aux[5:6, :] = lift
    aux[6:8, :] = jnp.zeros((2, NQ), f32)
    lse = best + jnp.log(total)
    tile = jnp.concatenate([lse[:, t * E : (t + 1) * E] for t in range(NQ // E)], axis=0)
    for k in range(NGROUP):
        lse_out[k] = tile


def row_scale(here, aux, lse_all, first, count):
    best = aux[0:1, pl.ds(first, count)]
    tiles = count // E
    if count == NQ:
        theirs = lse_all[...]
    else:
        theirs = jnp.concatenate(
            [lse_all[k, pl.ds(first // E, tiles), :][None] for k in range(NGROUP)], axis=0
        )
    mine = jnp.concatenate([best[:, t * E : (t + 1) * E] for t in range(tiles)], axis=0)
    member = lax.broadcasted_iota(i32, (NGROUP, tiles, E), 0)
    others = jnp.sum(jnp.where(member == here[2], 0.0, jnp.exp(theirs - mine[None])), axis=0)
    others = jnp.concatenate([others[t : t + 1, :] for t in range(tiles)], axis=1)
    weight = aux[2:3, pl.ds(first, count)]
    return weight / (aux[1:2, pl.ds(first, count)] + others)


def grad_kernel(shift, halves, here, c_ext, q_ext, aux, lse_all, *refs):
    n = len(halves)
    kept, refs = refs[: KEPT], refs[KEPT:]
    before = refs[: len(refs) - 1 - n]
    u_out, g_outs = refs[-1 - n], refs[-n:]
    u_in = before[0] if len(before) in (1, n + 1) and shift == 0 and halves == (0,) else None
    g_ins = before[-n:] if len(before) >= n and shift != 2 else [None] * n
    first = pl.multiple_of(((here[2] >> 3) - shift & 3) * QUART, QUART)
    span = pl.ds(first, QUART)
    scale = row_scale(here, aux, lse_all, first, QUART) * aux[5:6, span]
    queries = q_ext[span, :]
    narrow = queries[:, :E]
    base, weight = aux[4:5, span], aux[2:3, span]
    local = aux[3:4, span].astype(i32)
    total = jnp.zeros((QUART, E), f32) if u_in is None else u_in[...]
    for half, g_in, g_out in zip(halves, g_ins, g_outs):
        for k in range(NY):
            row = half * HALF + k * CB
            block = c_ext[row : row + CB, :]
            if half * NY + k < KEPT:
                expo = kept[half * NY + k][:, span] * scale
            else:
                logits = lax.dot_general(block, queries, NT, preferred_element_type=f32)
                expo = jnp.exp(logits - base) * scale
            matched = lax.broadcasted_iota(i32, expo.shape, 0) == (local - row)
            grad = (expo - jnp.where(matched, weight, 0.0)).astype(bf16)
            g_part = lax.dot_general(grad, narrow, NN, preferred_element_type=f32)
            g_out[k] = g_part if g_in is None else g_in[k] + g_part
            total = total + lax.dot_general(grad, block[:, :E], TN, preferred_element_type=f32)
    u_out[...] = total


def merge_kernel(own, came, *outs):
    for s, out in enumerate(outs):
        out[...] = own[s] + came[s]


def add_kernel(a, b, c, d, out):
    out[...] = (a[...] + b[...]) + (c[...] + d[...])


def ring(step):
    place = [(y & 1) * 2 + (y >> 1) for y in range(NY)]
    return [(place[y], place[(y + step) % NY]) for y in range(NY)]


def shaped(shape, dtype):
    return jax.ShapeDtypeStruct(shape, dtype)


def cost(pairs, products):
    return pl.CostEstimate(
        flops=pairs * E * products // 2, bytes_accessed=pairs, transcendentals=pairs // 8
    )


PARAMS = pltpu.CompilerParams(vmem_limit_bytes=18 * 2**20)


def per_device(queries, candidates, positive, bucket, query_weight, log_freq):
    y = lax.axis_index("yh") * 2 + lax.axis_index("yl")
    here = jnp.stack([y, lax.axis_index("c"), lax.axis_index(GROUP)]).astype(i32)

    q_block, c_block = pl.pallas_call(
        pack_kernel,
        out_shape=[shaped((NGROUP, QB + QPAD, E), bf16), shaped((CB + CPAD, E), bf16)],
        in_specs=[VMEM] * 5,
        out_specs=[VMEM] * 2,
        compiler_params=pltpu.CompilerParams(vmem_limit_bytes=60 * 2**20),
        name="pack",
    )(
        queries,
        positive.reshape(1, QB),
        query_weight.reshape(1, QB),
        candidates,
        bucket.reshape(4, E),
    )
    q_in = lax.all_to_all(q_block, GROUP, 0, 0, tiled=True)
    spread = [c_block]
    for s in range(1, NY):
        spread.append(lax.ppermute(c_block, RING, ring(s)))
    own = jnp.stack(spread)
    swap = [(0, 1), (1, 0)]
    other = lax.ppermute(own, "c", swap)

    table = jnp.tile(log_freq.reshape(SIDE, SIDE), (1, 4))

    c_ext, q_ext, aux, lse, *kept = pl.pallas_call(
        stats_kernel,
        out_shape=[
            shaped((NC, 2 * E), bf16),
            shaped((NQ, 2 * E), bf16),
            shaped((8, NQ), f32),
            shaped((NGROUP, NQ // E, E), f32),
        ]
        + [shaped((CB, NQ), f32)] * KEPT,
        in_specs=[SMEM] + [VMEM] * 4,
        out_specs=[VMEM] * (4 + KEPT),
        scratch_shapes=[pltpu.VMEM((8, NQ), f32)] * 3,
        compiler_params=PARAMS,
        cost_estimate=cost(NQ * NC, 1),
        name="stats",
    )(here, table, q_in, own, other)
    lse_all = lax.all_to_all(lse, GROUP, 0, 0, tiled=True)

    def grads(shift, halves, *extra, aliases):
        n = len(halves)
        return pl.pallas_call(
            functools.partial(grad_kernel, shift, halves),
            out_shape=[shaped((QUART, E), f32)] + [shaped((NY, CB, E), f32)] * n,
            in_specs=[SMEM] + [VMEM] * (4 + KEPT + len(extra)),
            out_specs=[VMEM] * (1 + n),
            input_output_aliases={i + KEPT: o for i, o in aliases.items()},
            compiler_params=PARAMS,
            cost_estimate=cost(QUART * HALF * n, 3),
            name="grad",
        )(here, c_ext, q_ext, aux, lse_all, *kept, *extra)

    def along_x(piece, shift):
        return lax.ppermute(piece, "x", [(i, (i - shift) % NX) for i in range(NX)])

    piece, g_a, g_b = grads(2, (0, 1), aliases={})
    u_two = along_x(piece, 2)
    piece, g_a, g_b = grads(1, (0, 1), g_a, g_b, aliases={5: 1, 6: 2})
    u_one = along_x(piece, 1)
    piece, g_a, g_b = grads(3, (0, 1), g_a, g_b, aliases={5: 1, 6: 2})
    u_three = along_x(piece, 3)
    u_two, g_b = lax.optimization_barrier((u_two, g_b))
    u_own, g_other = grads(0, (1,), g_b, aliases={5: 1})
    u_one, g_other = lax.optimization_barrier((u_one, g_other))
    g_came = lax.ppermute(g_other, "c", swap)
    u_own, g_own = grads(0, (0,), u_own, g_a, aliases={5: 0, 6: 1})

    u_line = pl.pallas_call(
        add_kernel,
        out_shape=shaped((QUART, E), f32),
        in_specs=[VMEM] * 4,
        out_specs=VMEM,
        compiler_params=PARAMS,
        cost_estimate=cost(NQ * NC, 150),
        name="add",
    )(u_two, u_one, u_three, u_own)
    u_line, g_own = lax.optimization_barrier((u_line, g_own))
    pieces = pl.pallas_call(
        merge_kernel,
        out_shape=[shaped((CB, E), f32)] * NY,
        in_specs=[VMEM] * 2,
        out_specs=[VMEM] * NY,
        compiler_params=PARAMS,
        name="merge",
    )(g_own, g_came)
    u_line, *pieces = lax.optimization_barrier((u_line, *pieces))
    for s in range(1, NY):
        pieces[s] = lax.ppermute(pieces[s], RING, ring(-s))
    u_in = lax.all_to_all(u_line.reshape(NZ, QB, E), "z", 0, 0, tiled=True)
    query_grad = jnp.sum(u_in, axis=0)
    cand_grad = (pieces[0] + pieces[1]) + (pieces[2] + pieces[3])
    return query_grad, cand_grad


def solution(mesh):
    fine = Mesh(mesh.devices.reshape(2, 2, 2, 4, 8), AXES)
    split = P(AXES)
    in_specs = (P(AXES, None), P(AXES, None), split, split, split, P())
    out_specs = (P(AXES, None), P(AXES, None))
    return jax.shard_map(
        per_device, mesh=fine, in_specs=in_specs, out_specs=out_specs, check_vma=False
    )
```

```python
import functools

import jax
import jax.numpy as jnp
from jax import lax
from jax.experimental import pallas as pl
from jax.experimental.pallas import tpu as pltpu
from jax.sharding import Mesh, PartitionSpec as P

bf16 = jnp.bfloat16
f32 = jnp.float32
i32 = jnp.int32
NT = (((1,), (1,)), ((), ()))
NN = (((1,), (0,)), ((), ()))
TN = (((0,), (0,)), ((), ()))
AXES = ("yl", "c", "yh", "x", "z")
GROUP = ("x", "z")
RING = ("yl", "yh")
NY, NX, NZ, NCORE = 4, 4, 8, 2
NGROUP = NX * NZ
VMEM = pl.BlockSpec(memory_space=pltpu.VMEM)
SMEM = pl.BlockSpec(memory_space=pltpu.SMEM)
E = 128
QB = 64
CB = 512
QPAD = 8
CPAD = 16
SIDE = 32
NQ = NGROUP * QB
HALF = NY * CB
QUART = NZ * QB
KEPT = 7
NC = NCORE * HALF


def pack_kernel(queries, positive, weight, candidates, bucket, q_out, c_out):
    place = positive[...]
    rows = [
        weight[...].astype(f32),
        (place >> 12).astype(f32),
        ((place >> 6) & 63).astype(f32),
        (place & 63).astype(f32),
        jnp.zeros((QPAD - 4, QB), f32),
    ]
    notes = jnp.concatenate(rows, axis=0)
    notes = jnp.concatenate([notes, notes], axis=1).astype(bf16)
    block = queries[...]
    for k in range(NGROUP):
        q_out[k, :QB, :] = block
        q_out[k, QB:, :] = notes
    codes = bucket[...]
    c_out[:CB, :] = candidates[...]
    c_out[CB:, :] = jnp.concatenate(
        [(codes >> 5).astype(f32), (codes & 31).astype(f32), jnp.zeros((CPAD - 8, E), f32)], axis=0
    ).astype(bf16)


def stats_kernel(here, table, q_in, own, other, c_ext, q_ext, aux, lse_out, *refs):
    kept, (meta, base_max, sums) = refs[:KEPT], refs[KEPT:]
    lane = lax.broadcasted_iota(i32, (SIDE, E), 1)
    row = lax.broadcasted_iota(i32, (SIDE, E), 0)
    freq = table[...]
    high = freq.astype(bf16).astype(f32)
    rest = freq - high
    middle = rest.astype(bf16).astype(f32)
    low = rest - middle
    parts = jnp.where(
        lane < SIDE, high, jnp.where(lane < 2 * SIDE, middle, jnp.where(lane < 3 * SIDE, low, 0.0))
    ).astype(bf16)
    pick = ((lane & (SIDE - 1)) == row).astype(f32).astype(bf16)

    for core, block_ref in enumerate((own, other)):
        for s in range(NY):
            first = core * HALF + s * CB
            c_ext[first : first + CB, :E] = block_ref[s, :CB, :]
            codes = block_ref[s, CB : CB + CPAD, :].astype(f32)
            for r in range(CB // E):
                major = codes[r : r + 1, :].astype(i32)
                minor = codes[4 + r : 5 + r, :].astype(i32)
                hot_major = (row == major).astype(f32).astype(bf16)
                hot_minor = (row == minor).astype(f32).astype(bf16)
                values = lax.dot_general(hot_major, parts, TN, preferred_element_type=f32)
                mask = lax.dot_general(hot_minor, pick, TN, preferred_element_type=f32)
                c_ext[first + r * E : first + (r + 1) * E, E:] = (-(values * mask)).astype(bf16)

    wide = lax.broadcasted_iota(i32, (8, E), 1)
    q_ext[:, E:] = jnp.ones((NQ, E), bf16)
    for k in range(NGROUP):
        q_ext[k * QB : (k + 1) * QB, :E] = q_in[k, :QB, :]
    for t in range(NGROUP // 2):
        even = q_in[2 * t, QB : QB + QPAD, :].astype(f32)
        odd = q_in[2 * t + 1, QB : QB + QPAD, :].astype(f32)
        meta[:, t * E : (t + 1) * E] = jnp.where(wide < QB, even, odd)
    weight = meta[0:1, :]
    position = (meta[1:2, :] * 4096.0 + meta[2:3, :] * 64.0 + meta[3:4, :]).astype(i32)
    block = position >> 9
    y_there = ((block >> 5) & 1) * 2 + ((block >> 7) & 1)
    c_there = (block >> 6) & 1
    slot = (c_there ^ here[1]) * NY + ((here[0] - y_there) & 3)
    local = jnp.where((block & 31) == here[2], slot * CB + (position & (CB - 1)), -1)
    aux[2:3, :] = weight
    aux[3:4, :] = local.astype(f32)

    rows = 512
    queries = q_ext[...]

    def tall(k):
        logits = lax.dot_general(
            c_ext[k * rows : (k + 1) * rows, :], queries, NT, preferred_element_type=f32
        )
        return logits.reshape(rows // 8, 8, NQ)

    def summed(k, logits):
        expo = jnp.exp(logits - base_max[...][None])
        if k < KEPT:
            kept[k][...] = expo.reshape(rows, NQ)
        return jnp.sum(expo, axis=0)

    block = tall(0)
    top = jnp.max(block, axis=0)
    base_max[...] = jnp.broadcast_to(jnp.max(top, axis=0, keepdims=True), (8, NQ))
    total = summed(0, block)
    for k in range(1, NC // rows):
        block = tall(k)
        top = jnp.maximum(top, jnp.max(block, axis=0))
        total = total + summed(k, block)
    sums[...] = total
    best = jnp.max(top, axis=0, keepdims=True)

    @pl.when(jnp.max(best - base_max[0:1, :]) > 40.0)
    def _():
        base_max[...] = jnp.broadcast_to(best, (8, NQ))
        again = summed(0, tall(0))
        for k in range(1, NC // rows):
            again = again + summed(k, tall(k))
        sums[...] = again

    base = base_max[0:1, :]
    lift = jnp.exp(base - best)
    total = jnp.sum(sums[...], axis=0, keepdims=True) * lift
    aux[0:1, :] = best
    aux[1:2, :] = total
    aux[4:5, :] = base
    aux[5:6, :] = lift
    aux[6:8, :] = jnp.zeros((2, NQ), f32)
    lse = best + jnp.log(total)
    tile = jnp.concatenate([lse[:, t * E : (t + 1) * E] for t in range(NQ // E)], axis=0)
    for k in range(NGROUP):
        lse_out[k] = tile


def row_scale(here, aux, lse_all, first, count):
    best = aux[0:1, pl.ds(first, count)]
    tiles = count // E
    if count == NQ:
        theirs = lse_all[...]
    else:
        theirs = jnp.concatenate(
            [lse_all[k, pl.ds(first // E, tiles), :][None] for k in range(NGROUP)], axis=0
        )
    mine = jnp.concatenate([best[:, t * E : (t + 1) * E] for t in range(tiles)], axis=0)
    member = lax.broadcasted_iota(i32, (NGROUP, tiles, E), 0)
    others = jnp.sum(jnp.where(member == here[2], 0.0, jnp.exp(theirs - mine[None])), axis=0)
    others = jnp.concatenate([others[t : t + 1, :] for t in range(tiles)], axis=1)
    weight = aux[2:3, pl.ds(first, count)]
    return weight / (aux[1:2, pl.ds(first, count)] + others)


def grad_kernel(shifts, halves, here, c_ext, q_ext, aux, lse_all, *refs):
    n, m = len(halves), len(shifts)
    kept, refs = refs[:KEPT], refs[KEPT:]
    before = refs[: len(refs) - m - n]
    u_outs, g_outs = refs[-m - n : -n], refs[-n:]
    u_in = before[0] if len(before) == n + 1 else None
    g_ins = before[-n:] if before else [None] * n
    rows = []
    for shift in shifts:
        first = pl.multiple_of(((here[2] >> 3) - shift & 3) * QUART, QUART)
        span = pl.ds(first, QUART)
        scale = row_scale(here, aux, lse_all, first, QUART) * aux[5:6, span]
        rows.append((span, scale, aux[4:5, span], aux[2:3, span], aux[3:4, span].astype(i32)))
    totals = [jnp.zeros((QUART, E), f32) if u_in is None else u_in[...] for _ in shifts]
    for half, g_in, g_out in zip(halves, g_ins, g_outs):
        for k in range(NY):
            row = half * HALF + k * CB
            block = c_ext[row : row + CB, :]
            g_sum = None if g_in is None else g_in[k]
            for t, (span, scale, base, weight, local) in enumerate(rows):
                queries = q_ext[span, :]
                if half * NY + k < KEPT:
                    expo = kept[half * NY + k][:, span] * scale
                else:
                    logits = lax.dot_general(block, queries, NT, preferred_element_type=f32)
                    expo = jnp.exp(logits - base) * scale
                matched = lax.broadcasted_iota(i32, expo.shape, 0) == (local - row)
                grad = (expo - jnp.where(matched, weight, 0.0)).astype(bf16)
                g_part = lax.dot_general(grad, queries[:, :E], NN, preferred_element_type=f32)
                g_sum = g_part if g_sum is None else g_sum + g_part
                totals[t] = totals[t] + lax.dot_general(
                    grad, block[:, :E], TN, preferred_element_type=f32
                )
            g_out[k] = g_sum
    for u_out, total in zip(u_outs, totals):
        u_out[...] = total


def merge_kernel(own, came, *outs):
    for s, out in enumerate(outs):
        out[...] = own[s] + came[s]


def add_kernel(a, b, c, d, out):
    out[...] = (a[...] + b[...]) + (c[...] + d[...])


def ring(step):
    place = [(y & 1) * 2 + (y >> 1) for y in range(NY)]
    return [(place[y], place[(y + step) % NY]) for y in range(NY)]


def shaped(shape, dtype):
    return jax.ShapeDtypeStruct(shape, dtype)


def cost(pairs, products):
    return pl.CostEstimate(
        flops=pairs * E * products // 2, bytes_accessed=pairs, transcendentals=pairs // 8
    )


PARAMS = pltpu.CompilerParams(vmem_limit_bytes=18 * 2**20)


def per_device(queries, candidates, positive, bucket, query_weight, log_freq):
    y = lax.axis_index("yh") * 2 + lax.axis_index("yl")
    here = jnp.stack([y, lax.axis_index("c"), lax.axis_index(GROUP)]).astype(i32)

    q_block, c_block = pl.pallas_call(
        pack_kernel,
        out_shape=[shaped((NGROUP, QB + QPAD, E), bf16), shaped((CB + CPAD, E), bf16)],
        in_specs=[VMEM] * 5,
        out_specs=[VMEM] * 2,
        compiler_params=pltpu.CompilerParams(vmem_limit_bytes=60 * 2**20),
        name="pack",
    )(
        queries,
        positive.reshape(1, QB),
        query_weight.reshape(1, QB),
        candidates,
        bucket.reshape(4, E),
    )
    q_in = lax.all_to_all(q_block, GROUP, 0, 0, tiled=True)
    spread = [c_block]
    for s in range(1, NY):
        spread.append(lax.ppermute(c_block, RING, ring(s)))
    own = jnp.stack(spread)
    swap = [(0, 1), (1, 0)]
    other = lax.ppermute(own, "c", swap)

    table = jnp.tile(log_freq.reshape(SIDE, SIDE), (1, 4))

    c_ext, q_ext, aux, lse, *kept = pl.pallas_call(
        stats_kernel,
        out_shape=[
            shaped((NC, 2 * E), bf16),
            shaped((NQ, 2 * E), bf16),
            shaped((8, NQ), f32),
            shaped((NGROUP, NQ // E, E), f32),
        ]
        + [shaped((CB, NQ), f32)] * KEPT,
        in_specs=[SMEM] + [VMEM] * 4,
        out_specs=[VMEM] * (4 + KEPT),
        scratch_shapes=[pltpu.VMEM((8, NQ), f32)] * 3,
        compiler_params=PARAMS,
        cost_estimate=cost(NQ * NC, 1),
        name="stats",
    )(here, table, q_in, own, other)
    lse_all = lax.all_to_all(lse, GROUP, 0, 0, tiled=True)

    def grads(shifts, halves, *extra, aliases):
        n = len(halves)
        return pl.pallas_call(
            functools.partial(grad_kernel, shifts, halves),
            out_shape=[shaped((QUART, E), f32)] * len(shifts) + [shaped((NY, CB, E), f32)] * n,
            in_specs=[SMEM] + [VMEM] * (4 + KEPT + len(extra)),
            out_specs=[VMEM] * (len(shifts) + n),
            input_output_aliases={i + KEPT: o for i, o in aliases.items()},
            compiler_params=PARAMS,
            cost_estimate=cost(QUART * HALF * n * len(shifts), 3),
            name="grad",
        )(here, c_ext, q_ext, aux, lse_all, *kept, *extra)

    def along_x(piece, shift):
        return lax.ppermute(piece, "x", [(i, (i - shift) % NX) for i in range(NX)])

    piece, g_a, g_b = grads((2,), (0, 1), aliases={})
    u_two = along_x(piece, 2)
    one, three, g_a, g_b = grads((1, 3), (0, 1), g_a, g_b, aliases={5: 2, 6: 3})
    u_one = along_x(one, 1)
    u_three = along_x(three, 3)
    u_two, g_b = lax.optimization_barrier((u_two, g_b))
    u_own, g_other = grads((0,), (1,), g_b, aliases={5: 1})
    g_came = lax.ppermute(g_other, "c", swap)
    u_own, g_own = grads((0,), (0,), u_own, g_a, aliases={5: 0, 6: 1})

    u_line = pl.pallas_call(
        add_kernel,
        out_shape=shaped((QUART, E), f32),
        in_specs=[VMEM] * 4,
        out_specs=VMEM,
        compiler_params=PARAMS,
        cost_estimate=cost(NQ * NC, 150),
        name="add",
    )(u_two, u_one, u_three, u_own)
    u_line, g_own = lax.optimization_barrier((u_line, g_own))
    pieces = pl.pallas_call(
        merge_kernel,
        out_shape=[shaped((CB, E), f32)] * NY,
        in_specs=[VMEM] * 2,
        out_specs=[VMEM] * NY,
        compiler_params=PARAMS,
        name="merge",
    )(g_own, g_came)
    u_line, *pieces = lax.optimization_barrier((u_line, *pieces))
    for s in range(1, NY):
        pieces[s] = lax.ppermute(pieces[s], RING, ring(-s))
    u_in = lax.all_to_all(u_line.reshape(NZ, QB, E), "z", 0, 0, tiled=True)
    query_grad = jnp.sum(u_in, axis=0)
    cand_grad = (pieces[0] + pieces[1]) + (pieces[2] + pieces[3])
    return query_grad, cand_grad


def solution(mesh):
    fine = Mesh(mesh.devices.reshape(2, 2, 2, 4, 8), AXES)
    split = P(AXES)
    in_specs = (P(AXES, None), P(AXES, None), split, split, split, P())
    out_specs = (P(AXES, None), P(AXES, None))
    return jax.shard_map(
        per_device, mesh=fine, in_specs=in_specs, out_specs=out_specs, check_vma=False
    )
```

```python
import functools

import jax
import jax.numpy as jnp
from jax import lax
from jax.experimental import pallas as pl
from jax.experimental.pallas import tpu as pltpu
from jax.sharding import Mesh, PartitionSpec as P

bf16 = jnp.bfloat16
f32 = jnp.float32
i32 = jnp.int32
NT = (((1,), (1,)), ((), ()))
NN = (((1,), (0,)), ((), ()))
TN = (((0,), (0,)), ((), ()))
AXES = ("yl", "c", "yh", "x", "z")
GROUP = ("x", "z")
RING = ("yl", "yh")
NY, NX, NZ, NCORE = 4, 4, 8, 2
NGROUP = NX * NZ
VMEM = pl.BlockSpec(memory_space=pltpu.VMEM)
SMEM = pl.BlockSpec(memory_space=pltpu.SMEM)
E = 128
QB = 64
CB = 512
QPAD = 8
CPAD = 16
SIDE = 32
NQ = NGROUP * QB
HALF = NY * CB
QUART = NZ * QB
KEPT = 7
NC = NCORE * HALF


def pack_kernel(queries, positive, weight, candidates, bucket, q_out, c_out):
    place = positive[...]
    rows = [
        weight[...].astype(f32),
        (place >> 12).astype(f32),
        ((place >> 6) & 63).astype(f32),
        (place & 63).astype(f32),
        jnp.zeros((QPAD - 4, QB), f32),
    ]
    notes = jnp.concatenate(rows, axis=0)
    notes = jnp.concatenate([notes, notes], axis=1).astype(bf16)
    block = queries[...]
    for k in range(NGROUP):
        q_out[k, :QB, :] = block
        q_out[k, QB:, :] = notes
    codes = bucket[...]
    c_out[:CB, :] = candidates[...]
    c_out[CB:, :] = jnp.concatenate(
        [(codes >> 5).astype(f32), (codes & 31).astype(f32), jnp.zeros((CPAD - 8, E), f32)], axis=0
    ).astype(bf16)


def stats_kernel(here, table, q_in, own, other, c_ext, q_ext, aux, lse_out, *refs):
    kept, (meta, base_max, sums) = refs[:KEPT], refs[KEPT:]
    lane = lax.broadcasted_iota(i32, (SIDE, E), 1)
    row = lax.broadcasted_iota(i32, (SIDE, E), 0)
    freq = table[...]
    high = freq.astype(bf16).astype(f32)
    rest = freq - high
    middle = rest.astype(bf16).astype(f32)
    low = rest - middle
    parts = jnp.where(
        lane < SIDE, high, jnp.where(lane < 2 * SIDE, middle, jnp.where(lane < 3 * SIDE, low, 0.0))
    ).astype(bf16)
    pick = ((lane & (SIDE - 1)) == row).astype(f32).astype(bf16)

    for core, block_ref in enumerate((own, other)):
        for s in range(NY):
            first = core * HALF + s * CB
            c_ext[first : first + CB, :E] = block_ref[s, :CB, :]
            codes = block_ref[s, CB : CB + CPAD, :].astype(f32)
            for r in range(CB // E):
                major = codes[r : r + 1, :].astype(i32)
                minor = codes[4 + r : 5 + r, :].astype(i32)
                hot_major = (row == major).astype(f32).astype(bf16)
                hot_minor = (row == minor).astype(f32).astype(bf16)
                values = lax.dot_general(hot_major, parts, TN, preferred_element_type=f32)
                mask = lax.dot_general(hot_minor, pick, TN, preferred_element_type=f32)
                c_ext[first + r * E : first + (r + 1) * E, E:] = (-(values * mask)).astype(bf16)

    wide = lax.broadcasted_iota(i32, (8, E), 1)
    q_ext[:, E:] = jnp.ones((NQ, E), bf16)
    for k in range(NGROUP):
        q_ext[k * QB : (k + 1) * QB, :E] = q_in[k, :QB, :]
    for t in range(NGROUP // 2):
        even = q_in[2 * t, QB : QB + QPAD, :].astype(f32)
        odd = q_in[2 * t + 1, QB : QB + QPAD, :].astype(f32)
        meta[:, t * E : (t + 1) * E] = jnp.where(wide < QB, even, odd)
    weight = meta[0:1, :]
    position = (meta[1:2, :] * 4096.0 + meta[2:3, :] * 64.0 + meta[3:4, :]).astype(i32)
    block = position >> 9
    y_there = ((block >> 5) & 1) * 2 + ((block >> 7) & 1)
    c_there = (block >> 6) & 1
    slot = (c_there ^ here[1]) * NY + ((here[0] - y_there) & 3)
    local = jnp.where((block & 31) == here[2], slot * CB + (position & (CB - 1)), -1)
    aux[2:3, :] = weight
    aux[3:4, :] = local.astype(f32)

    rows = 512
    queries = q_ext[...]

    def tall(k):
        logits = lax.dot_general(
            c_ext[k * rows : (k + 1) * rows, :], queries, NT, preferred_element_type=f32
        )
        return logits.reshape(rows // 8, 8, NQ)

    def summed(k, logits):
        expo = jnp.exp(logits - base_max[...][None])
        if k < KEPT:
            kept[k][...] = expo.reshape(rows, NQ)
        return jnp.sum(expo, axis=0)

    block = tall(0)
    top = jnp.max(block, axis=0)
    base_max[...] = jnp.broadcast_to(jnp.max(top, axis=0, keepdims=True), (8, NQ))
    total = summed(0, block)
    for k in range(1, NC // rows):
        block = tall(k)
        top = jnp.maximum(top, jnp.max(block, axis=0))
        total = total + summed(k, block)
    sums[...] = total
    best = jnp.max(top, axis=0, keepdims=True)

    @pl.when(jnp.max(best - base_max[0:1, :]) > 40.0)
    def _():
        base_max[...] = jnp.broadcast_to(best, (8, NQ))
        again = summed(0, tall(0))
        for k in range(1, NC // rows):
            again = again + summed(k, tall(k))
        sums[...] = again

    base = base_max[0:1, :]
    lift = jnp.exp(base - best)
    total = jnp.sum(sums[...], axis=0, keepdims=True) * lift
    aux[0:1, :] = best
    aux[1:2, :] = total
    aux[4:5, :] = base
    aux[5:6, :] = lift
    aux[6:8, :] = jnp.zeros((2, NQ), f32)
    lse = best + jnp.log(total)
    tile = jnp.concatenate([lse[:, t * E : (t + 1) * E] for t in range(NQ // E)], axis=0)
    for k in range(NGROUP):
        lse_out[k] = tile


def row_scale(here, aux, lse_all, first, count):
    best = aux[0:1, pl.ds(first, count)]
    tiles = count // E
    if count == NQ:
        theirs = lse_all[...]
    else:
        theirs = jnp.concatenate(
            [lse_all[k, pl.ds(first // E, tiles), :][None] for k in range(NGROUP)], axis=0
        )
    mine = jnp.concatenate([best[:, t * E : (t + 1) * E] for t in range(tiles)], axis=0)
    member = lax.broadcasted_iota(i32, (NGROUP, tiles, E), 0)
    others = jnp.sum(jnp.where(member == here[2], 0.0, jnp.exp(theirs - mine[None])), axis=0)
    others = jnp.concatenate([others[t : t + 1, :] for t in range(tiles)], axis=1)
    weight = aux[2:3, pl.ds(first, count)]
    return weight / (aux[1:2, pl.ds(first, count)] + others)


def grad_kernel(shifts, halves, here, c_ext, q_ext, aux, lse_all, *refs):
    n, m = len(halves), len(shifts)
    kept, refs = refs[:KEPT], refs[KEPT:]
    before = refs[: len(refs) - m - n]
    u_outs, g_outs = refs[-m - n : -n], refs[-n:]
    u_in = before[0] if len(before) == n + 1 else None
    g_ins = before[-n:] if before else [None] * n
    rows = []
    for shift in shifts:
        first = pl.multiple_of(((here[2] >> 3) - shift & 3) * QUART, QUART)
        span = pl.ds(first, QUART)
        scale = row_scale(here, aux, lse_all, first, QUART) * aux[5:6, span]
        rows.append((span, scale, aux[4:5, span], aux[2:3, span], aux[3:4, span].astype(i32)))
    totals = [jnp.zeros((QUART, E), f32) if u_in is None else u_in[...] for _ in shifts]
    for half, g_in, g_out in zip(halves, g_ins, g_outs):
        for k in range(NY):
            row = half * HALF + k * CB
            block = c_ext[row : row + CB, :]
            g_sum = None if g_in is None else g_in[k]
            for t, (span, scale, base, weight, local) in enumerate(rows):
                queries = q_ext[span, :]
                if half * NY + k < KEPT:
                    expo = kept[half * NY + k][:, span] * scale
                else:
                    logits = lax.dot_general(block, queries, NT, preferred_element_type=f32)
                    expo = jnp.exp(logits - base) * scale
                matched = lax.broadcasted_iota(i32, expo.shape, 0) == (local - row)
                grad = (expo - jnp.where(matched, weight, 0.0)).astype(bf16)
                g_part = lax.dot_general(grad, queries[:, :E], NN, preferred_element_type=f32)
                g_sum = g_part if g_sum is None else g_sum + g_part
                totals[t] = totals[t] + lax.dot_general(
                    grad, block[:, :E], TN, preferred_element_type=f32
                )
            g_out[k] = g_sum
    for u_out, total in zip(u_outs, totals):
        u_out[...] = total


def merge_kernel(own, came, *outs):
    for s, out in enumerate(outs):
        out[...] = own[s] + came[s]


def add_kernel(a, b, c, d, out):
    out[...] = (a[...] + b[...]) + (c[...] + d[...])


def ring(step):
    place = [(y & 1) * 2 + (y >> 1) for y in range(NY)]
    return [(place[y], place[(y + step) % NY]) for y in range(NY)]


def shaped(shape, dtype):
    return jax.ShapeDtypeStruct(shape, dtype)


def cost(pairs, products):
    return pl.CostEstimate(
        flops=pairs * E * products // 2, bytes_accessed=pairs, transcendentals=pairs // 8
    )


PARAMS = pltpu.CompilerParams(vmem_limit_bytes=18 * 2**20)


def per_device(queries, candidates, positive, bucket, query_weight, log_freq):
    y = lax.axis_index("yh") * 2 + lax.axis_index("yl")
    here = jnp.stack([y, lax.axis_index("c"), lax.axis_index(GROUP)]).astype(i32)

    q_block, c_block = pl.pallas_call(
        pack_kernel,
        out_shape=[shaped((NGROUP, QB + QPAD, E), bf16), shaped((CB + CPAD, E), bf16)],
        in_specs=[VMEM] * 5,
        out_specs=[VMEM] * 2,
        compiler_params=pltpu.CompilerParams(vmem_limit_bytes=60 * 2**20),
        name="pack",
    )(
        queries,
        positive.reshape(1, QB),
        query_weight.reshape(1, QB),
        candidates,
        bucket.reshape(4, E),
    )
    q_in = lax.all_to_all(q_block, GROUP, 0, 0, tiled=True)
    spread = [c_block]
    for s in range(1, NY):
        spread.append(lax.ppermute(c_block, RING, ring(s)))
    own = jnp.stack(spread)
    swap = [(0, 1), (1, 0)]
    other = lax.ppermute(own, "c", swap)

    table = jnp.tile(log_freq.reshape(SIDE, SIDE), (1, 4))

    c_ext, q_ext, aux, lse, *kept = pl.pallas_call(
        stats_kernel,
        out_shape=[
            shaped((NC, 2 * E), bf16),
            shaped((NQ, 2 * E), bf16),
            shaped((8, NQ), f32),
            shaped((NGROUP, NQ // E, E), f32),
        ]
        + [shaped((CB, NQ), f32)] * KEPT,
        in_specs=[SMEM] + [VMEM] * 4,
        out_specs=[VMEM] * (4 + KEPT),
        scratch_shapes=[pltpu.VMEM((8, NQ), f32)] * 3,
        compiler_params=PARAMS,
        cost_estimate=cost(NQ * NC, 1),
        name="stats",
    )(here, table, q_in, own, other)
    lse_all = lax.all_to_all(lse, GROUP, 0, 0, tiled=True)

    def grads(shifts, halves, *extra, aliases):
        n = len(halves)
        return pl.pallas_call(
            functools.partial(grad_kernel, shifts, halves),
            out_shape=[shaped((QUART, E), f32)] * len(shifts) + [shaped((NY, CB, E), f32)] * n,
            in_specs=[SMEM] + [VMEM] * (4 + KEPT + len(extra)),
            out_specs=[VMEM] * (len(shifts) + n),
            input_output_aliases={i + KEPT: o for i, o in aliases.items()},
            compiler_params=PARAMS,
            cost_estimate=cost(QUART * HALF * n * len(shifts), 3),
            name="grad",
        )(here, c_ext, q_ext, aux, lse_all, *kept, *extra)

    def along_x(piece, shift):
        return lax.ppermute(piece, "x", [(i, (i - shift) % NX) for i in range(NX)])

    piece, g_a, g_b = grads((2,), (0, 1), aliases={})
    u_two = along_x(piece, 2)
    one, three, g_a, g_b = grads((1, 3), (0, 1), g_a, g_b, aliases={5: 2, 6: 3})
    u_one = along_x(one, 1)
    u_three = along_x(three, 3)
    u_two, g_b = lax.optimization_barrier((u_two, g_b))
    u_own, g_other = grads((0,), (1,), g_b, aliases={5: 1})
    g_came = lax.ppermute(g_other, "c", swap)
    u_own, g_own = grads((0,), (0,), u_own, g_a, aliases={5: 0, 6: 1})

    u_line = pl.pallas_call(
        add_kernel,
        out_shape=shaped((QUART, E), f32),
        in_specs=[VMEM] * 4,
        out_specs=VMEM,
        compiler_params=PARAMS,
        cost_estimate=cost(NQ * NC, 150),
        name="add",
    )(u_two, u_one, u_three, u_own)
    u_line, g_own = lax.optimization_barrier((u_line, g_own))
    pieces = pl.pallas_call(
        merge_kernel,
        out_shape=[shaped((CB, E), f32)] * NY,
        in_specs=[VMEM] * 2,
        out_specs=[VMEM] * NY,
        compiler_params=PARAMS,
        name="merge",
    )(g_own, g_came)
    u_line, *pieces = lax.optimization_barrier((u_line, *pieces))
    for s in (2, 1, 3):
        pieces[s] = lax.ppermute(pieces[s], RING, ring(-s))
    u_in = lax.all_to_all(u_line.reshape(NZ, QB, E), "z", 0, 0, tiled=True)
    query_grad = jnp.sum(u_in, axis=0)
    cand_grad = (pieces[0] + pieces[1]) + (pieces[2] + pieces[3])
    return query_grad, cand_grad


def solution(mesh):
    fine = Mesh(mesh.devices.reshape(2, 2, 2, 4, 8), AXES)
    split = P(AXES)
    in_specs = (P(AXES, None), P(AXES, None), split, split, split, P())
    out_specs = (P(AXES, None), P(AXES, None))
    return jax.shard_map(
        per_device, mesh=fine, in_specs=in_specs, out_specs=out_specs, check_vma=False
    )
```
